128 devices in a mesh: node: 16 (over x, z), local: 8 (over y, core).
Axes of the slice: x: 4, y: 4, z: 4, core: 2. Of those that a mesh axis runs over, the one named last changes fastest.
Arguments:
- activations: bfloat16 [16384, 2048], P(('node', 'local')), may hold values from -6 to 6
- expert_ids: int32 [16384, 8], P(('node', 'local')), may hold values from 0 to 127, as said below
- route_gates: bfloat16 [16384, 8], P(('node', 'local')), may hold values from 0.19921875 to 0.796875
- gate_proj: bfloat16 [128, 2048, 768], P(('node', 'local')), may hold values from -0.125 to 0.125
- up_proj: bfloat16 [128, 2048, 768], P(('node', 'local')), may hold values from -0.125 to 0.125
- down_proj: bfloat16 [128, 768, 2048], P(('node', 'local')), may hold values from -0.21875 to 0.21875
Outputs:
- moe_out: bfloat16 [16384, 2048], P(('node', 'local'))
The draws below stay inside these ranges and needn't reach their ends.
Inputs may be any that keep to these rules, and one draw needn't show every extreme that they name: `expert_ids`: group k holds experts k * 8 to k * 8 + 7. Entries 2i and 2i+1 of a token's list name two different experts of one group, and a token's pairs name 4 different groups. Of the 128 tokens of one device (aligned blocks of rows), exactly 32 choose each group. Each group has one expert, its busiest, that is named by exactly 16 tokens of every device; every other expert is named by at most 8 tokens of one device, and in each block some expert of each group is named by exactly 8.
All inputs are finite; a program needn't handle non-finite values.
Results may differ from the reference program's by a relative error of at most 0.012.
Values may be sent and summed in bfloat16 or wider, within the bound.
No kernel may reach another device: no remote copies, remote signals or barrier semaphores. Data moves between devices by JAX's collectives and lax.ppermute only.
A program may use at most 128 MiB of HBM per device.

```python
import jax
import jax.numpy as jnp
from jax import lax

D = 2048
FF = 768
TOP = 8
NODES_TOK = 4
TOK_DEV = 128
NODES = 16
EXP_NODE = 8
EXPERTS = 128
TOKENS = 16384
NODE_ROWS = 32
MOST = 16
COLD_MOST = 8


def group_counts(sub_key):
    remaining = 2 * NODE_ROWS - MOST
    rest = remaining - COLD_MOST
    share = rest // (EXP_NODE - 2)
    extra = rest - share * (EXP_NODE - 2)
    order = jax.random.permutation(sub_key, EXP_NODE - 2).astype(jnp.int32)
    others = share + (order < extra).astype(jnp.int32)
    cold = jnp.concatenate([jnp.full((1,), COLD_MOST, jnp.int32), others.astype(jnp.int32)])
    cold = cold[jax.random.permutation(jax.random.fold_in(sub_key, 7), EXP_NODE - 1)]
    return jnp.concatenate([jnp.full((1,), MOST, jnp.int32), cold.astype(jnp.int32)])


def group_locals(sub_key, hot_local):
    counts = group_counts(sub_key)
    group_ends = jnp.cumsum(counts)
    position = jnp.arange(2 * NODE_ROWS, dtype=jnp.int32)
    order_rank = jnp.sum((position[:, None] >= group_ends[None, :]).astype(jnp.int32), axis=1)
    return ((hot_local + order_rank) % EXP_NODE).astype(jnp.int32)


def group_shuffle(sub_key):
    return jax.random.permutation(jax.random.fold_in(sub_key, 5), NODE_ROWS).astype(jnp.int32)


def block_lists(block_key, hot_local):
    sub_keys = jax.random.split(block_key, 4)
    token_order = jax.random.permutation(sub_keys[0], TOK_DEV).astype(jnp.int32)
    node_order = jax.random.permutation(sub_keys[1], NODES).astype(jnp.int32)
    offsets = jax.random.permutation(sub_keys[2], NODES).astype(jnp.int32)[:NODES_TOK]
    node_keys = jax.random.split(sub_keys[3], NODES)
    sequences = jax.vmap(group_locals)(node_keys, hot_local)
    shuffles = jax.vmap(group_shuffle)(node_keys)
    pair_index = jnp.arange(NODES_TOK, dtype=jnp.int32)
    chosen_node = node_order[(token_order[:, None] + offsets[None, :]) % NODES]
    group_index = pair_index[None, :] * (TOK_DEV // NODES) + token_order[:, None] // NODES
    shuffled = shuffles[chosen_node, group_index]
    first_local = sequences[chosen_node, shuffled]
    second_local = sequences[chosen_node, shuffled + NODE_ROWS]
    lists = jnp.stack([chosen_node * EXP_NODE + first_local, chosen_node * EXP_NODE + second_local], axis=2)
    return lists.reshape(TOK_DEV, TOP)


def draw_expert_ids(key, part):
    key = jax.random.fold_in(key, 3)
    hot_local = jax.random.randint(jax.random.fold_in(key, 1), (NODES,), 0, EXP_NODE).astype(jnp.int32)
    block_keys = jax.random.split(jax.random.fold_in(key, 2), TOKENS // TOK_DEV)
    lists = jax.vmap(block_lists, in_axes=(0, None))(block_keys, hot_local)
    return lists.reshape(TOKENS, TOP).astype(jnp.int32)


def shard_levels(own_key, shape, cuts, smallest, top_value):
    def one(dim, shards_of):
        steps = jax.random.uniform(jax.random.fold_in(jax.random.fold_in(own_key, 6), dim), (shards_of,), jnp.float32, smallest / len(cuts), top_value / len(cuts))
        return jnp.repeat(jnp.exp(steps), shape[dim] // shards_of).reshape((-1,) + (1,) * (len(shape) - dim - 1))

    factor_of = one(*cuts[0])
    for cut in cuts[1:]:
        factor_of = factor_of * one(*cut)
    return factor_of


def bell_draw(own_key, dims, scale, reach, pieces=(), kind=jnp.bfloat16):
    entries = jax.random.normal(own_key, dims, jnp.float32) * scale
    if len(pieces) > 0:
        entries = shard_levels(own_key, dims, pieces, -0.22, 0.18) * entries
    return jnp.clip(entries, min=-reach, max=reach).astype(kind)


def setup_inputs(seed: int = 0) -> dict:
    key_of = jax.random.split(jax.random.key(seed), 7)
    activations = bell_draw(key_of[0], (TOKENS, D), 1.0, 6.0, ((0, 128),))
    expert_ids = draw_expert_ids(jax.random.fold_in(key_of[6], 71), 0)
    route_gates = jnp.clip(0.19921875 + 0.59765625 * jax.random.uniform(key_of[2], (TOKENS, TOP), jnp.float32) ** shard_levels(key_of[2], (TOKENS, TOP), ((0, 128),), -0.2, 0.2), 0.19921875, 0.796875).astype(jnp.bfloat16)
    gate_proj = bell_draw(key_of[3], (EXPERTS, D, FF), D ** -0.5, 0.125, ((0, 128),))
    up_proj = bell_draw(key_of[4], (EXPERTS, D, FF), D ** -0.5, 0.125, ((0, 128),))
    down_proj = bell_draw(key_of[5], (EXPERTS, FF, D), FF ** -0.5, 0.21875, ((0, 128),))
    return {"activations": activations, "expert_ids": expert_ids, "route_gates": route_gates, "gate_proj": gate_proj, "up_proj": up_proj, "down_proj": down_proj}


def reference(activations, expert_ids, route_gates, gate_proj, up_proj, down_proj):
    tokens_all = activations.shape[0]
    model_width = activations.shape[1]
    blocks = tokens_all // TOK_DEV
    experts = gate_proj.shape[0]
    picks_all = tokens_all * TOP
    block_ids = expert_ids.reshape(blocks, TOK_DEV * TOP)
    labels = jnp.arange(experts, dtype=jnp.int32)

    def block_ranks(block_row):
        onehot = (block_row[:, None] == labels[None, :]).astype(jnp.int32)
        return jnp.sum(jnp.cumsum(onehot, axis=0) * onehot, axis=1) - 1

    slot_ranks = jax.vmap(block_ranks)(block_ids)
    slot_index = (jnp.arange(blocks, dtype=jnp.int32)[:, None] * MOST + slot_ranks).reshape(-1).astype(jnp.int32)
    pick_table = jnp.full((experts, blocks * MOST), picks_all, jnp.int32)
    pick_table = pick_table.at[expert_ids.reshape(-1), slot_index].set(jnp.arange(picks_all, dtype=jnp.int32))
    padded = jnp.concatenate([activations, jnp.zeros((1, model_width), activations.dtype)], axis=0)

    def one_expert(carried, inputs):
        index_row, gate_w, up_w, down_w = inputs
        gathered = padded[index_row // TOP]
        gate_h = jnp.dot(gathered, gate_w, preferred_element_type=jnp.float32)
        up_h = jnp.dot(gathered, up_w, preferred_element_type=jnp.float32)
        hidden_act = (jax.nn.silu(gate_h) * up_h).astype(jnp.bfloat16)
        expert_out = jnp.dot(hidden_act, down_w, preferred_element_type=jnp.float32).astype(jnp.bfloat16)
        carried = carried.at[index_row].set(expert_out, mode="drop")
        return carried, None

    pick_outs, _ = lax.scan(one_expert, jnp.zeros((picks_all, model_width), jnp.bfloat16),
                            (pick_table, gate_proj, up_proj, down_proj))
    gate_vals = route_gates.reshape(tokens_all, NODES_TOK, 2).astype(jnp.float32)
    weighted = gate_vals[:, :, :, None] * pick_outs.reshape(tokens_all, NODES_TOK, 2, model_width).astype(jnp.float32)
    pair_sum = jnp.sum(weighted, axis=2).astype(jnp.bfloat16)
    return jnp.sum(pair_sum.astype(jnp.float32), axis=1).astype(jnp.bfloat16)
```

```python
import functools

import jax
import jax.numpy as jnp
from jax import lax
from jax.experimental import pallas as pl
from jax.experimental.pallas import tpu as pltpu
from jax.sharding import PartitionSpec as P

SLOTS = 8
SHIFT = 3
BF16 = jnp.bfloat16
F32 = jnp.float32
VMEM_BYTES = 48 * 1024 * 1024


def iota(shape, dim):
    return lax.broadcasted_iota(jnp.int32, shape, dim)


def indicator(mask):
    return jnp.where(mask, 1.0, 0.0).astype(F32)


def dot(left, right):
    return jnp.dot(left, right, preferred_element_type=F32)


def ranks_of(named):
    tokens = named.shape[1]
    earlier = indicator(iota((tokens, tokens), 0) < iota((tokens, tokens), 1))
    return dot(named.astype(BF16), earlier.astype(BF16))


def spread(values, slots):
    labels = values.shape[0]
    picks = indicator((iota((labels * slots, labels), 0) >> SHIFT) == iota((labels * slots, labels), 1))
    return dot(picks.astype(BF16), values.astype(BF16))


def group_sums(values, groups):
    experts = values.shape[0]
    per_group = experts // groups
    shape = (groups * SLOTS, experts)
    same = indicator((iota(shape, 0) >> SHIFT) == (iota(shape, 1) // per_group))
    return dot(same.astype(BF16), values.astype(BF16))


def marks_of(ids_ref, labels):
    total = indicator(labels == ids_ref[0:1, :])
    for entry in range(1, ids_ref.shape[0]):
        total = total + indicator(labels == ids_ref[entry : entry + 1, :])
    return total


def spill_codes(named, ranks):
    return named * jnp.maximum(ranks - (SLOTS - 1), 0.0)


def spill_kernel(groups, experts, ids_ref, acts_ref, out_ref):
    tokens = ids_ref.shape[1]
    named = marks_of(ids_ref, iota((experts, tokens), 0))
    codes = group_sums(spill_codes(named, ranks_of(named)), groups)
    slot = (iota(codes.shape, 0) & (SLOTS - 1)).astype(F32)
    out_ref[...] = dot(indicator(codes == slot + 1.0).astype(BF16), acts_ref[...]).astype(BF16)


def weight_kernel(groups, experts, ids_ref, gates_ref, main_ref, spill_ref):
    tokens = ids_ref.shape[1]
    labels = iota((experts, tokens), 0)
    named = marks_of(ids_ref, labels)
    gates = jnp.zeros((experts, tokens), F32)
    for entry in range(ids_ref.shape[0]):
        value = gates_ref[entry : entry + 1, :].astype(F32)
        gates = gates + jnp.where(labels == ids_ref[entry : entry + 1, :], value, 0.0)
    ranks = ranks_of(named)
    rank_rows = spread(jnp.where(named > 0.0, ranks, 99.0), SLOTS)
    gate_rows = spread(gates, SLOTS)
    slot = (iota(rank_rows.shape, 0) & (SLOTS - 1)).astype(F32)
    main_ref[...] = jnp.where(rank_rows == slot, gate_rows, 0.0).astype(BF16)
    codes = spill_codes(named, ranks)
    code_rows = group_sums(codes, groups)
    spill_rows = group_sums(jnp.where(codes > 0.0, gates, 0.0), groups)
    spill_slot = (iota(code_rows.shape, 0) & (SLOTS - 1)).astype(F32)
    spill_ref[...] = jnp.where(code_rows == spill_slot + 1.0, spill_rows, 0.0).astype(BF16)


def gather_kernel(groups, per_group, my_ref, ids_ref, acts_ref, out_ref):
    tokens = ids_ref.shape[1]
    named = marks_of(ids_ref, iota((groups, tokens), 0) * per_group + my_ref[0])
    rank_rows = spread(jnp.where(named > 0.0, ranks_of(named), 99.0), SLOTS)
    slot = (iota(rank_rows.shape, 0) & (SLOTS - 1)).astype(F32)
    rows = dot(indicator(rank_rows == slot).astype(BF16), acts_ref[...])
    out_ref[...] = rows.reshape(groups, 1, SLOTS, rows.shape[1]).astype(BF16)


def expert_kernel(on_ref, rows_ref, gate_hbm, up_hbm, down_hbm, out_ref, gate_w, up_w, down_w, sems):
    step = pl.program_id(0)
    busy = on_ref[0] != 0
    copies = [
        pltpu.make_async_copy(source.at[0], target, sems.at[place])
        for place, (source, target) in enumerate(((gate_hbm, gate_w), (up_hbm, up_w), (down_hbm, down_w)))
    ]

    @pl.when(busy & (step == 0))
    def _():
        for copy in copies:
            copy.start()

    def arrived(place):
        @pl.when(step == 0)
        def _():
            copies[place].wait()

    @pl.when(busy)
    def _():
        rows = rows_ref[...]
        arrived(0)
        gate_h = dot(rows, gate_w[...])
        arrived(1)
        up_h = dot(rows, up_w[...])
        hidden = (gate_h / (1.0 + jnp.exp(-gate_h)) * up_h).astype(BF16)
        arrived(2)
        out_ref[...] = dot(hidden, down_w[...]).astype(BF16)

    @pl.when(jnp.logical_not(busy))
    def _():
        out_ref[...] = jnp.zeros(out_ref.shape, BF16)


def combine_kernel(main_w_ref, spill_w_ref, main_ref, spill_ref, out_ref):
    over_rows = (((0,), (0,)), ((), ()))
    total = lax.dot_general(main_w_ref[...], main_ref[...], over_rows, preferred_element_type=F32)
    total += lax.dot_general(spill_w_ref[...], spill_ref[...], over_rows, preferred_element_type=F32)
    out_ref[...] = total.astype(BF16)


def params():
    return pltpu.CompilerParams(vmem_limit_bytes=VMEM_BYTES)


def whole():
    return pl.BlockSpec(memory_space=pltpu.VMEM)


def scalar():
    return pl.BlockSpec(memory_space=pltpu.SMEM)


def apply_expert(on, rows, gate_proj, up_proj, down_proj):
    count, width = rows.shape
    hidden = gate_proj.shape[2]
    block = min(256, count)
    anywhere = pl.BlockSpec(memory_space=pl.ANY)
    return pl.pallas_call(
        expert_kernel,
        grid=(count // block,),
        in_specs=[scalar(), pl.BlockSpec((block, width), lambda i: (i, 0)), anywhere, anywhere, anywhere],
        out_specs=pl.BlockSpec((block, width), lambda i: (i, 0)),
        out_shape=jax.ShapeDtypeStruct((count, width), BF16),
        scratch_shapes=[
            pltpu.VMEM((width, hidden), BF16),
            pltpu.VMEM((width, hidden), BF16),
            pltpu.VMEM((hidden, width), BF16),
            pltpu.SemaphoreType.DMA((3,)),
        ],
        compiler_params=params(),
        cost_estimate=pl.CostEstimate(
            flops=6 * count * width * hidden,
            bytes_accessed=4 * count * width + 6 * width * hidden,
            transcendentals=count * hidden,
        ),
        name="expert",
    )(on, rows, gate_proj, up_proj, down_proj)


def shards(activations, expert_ids, route_gates, gate_proj, up_proj, down_proj):
    tokens, width = activations.shape
    top = expert_ids.shape[1]
    groups = lax.axis_size("node")
    per_group = lax.axis_size("local")
    experts = groups * per_group
    my_local = lax.axis_index("local").astype(jnp.int32)
    my_expert = lax.axis_index("node").astype(jnp.int32) * per_group + my_local
    id_rows = expert_ids.T
    gate_rows = route_gates.T

    acts_all = lax.all_gather(activations, "local", tiled=True)
    ids_all = lax.all_gather(id_rows, "local", tiled=True)

    spill = pl.pallas_call(
        functools.partial(spill_kernel, groups, experts),
        in_specs=[whole(), whole()],
        out_specs=whole(),
        out_shape=jax.ShapeDtypeStruct((groups * SLOTS, width), BF16),
        compiler_params=params(),
        name="spill_rows",
    )(id_rows, activations)
    spill_in = lax.all_to_all(spill.reshape(groups, SLOTS, width), "node", split_axis=0, concat_axis=0, tiled=True)
    spill_all = lax.all_gather(spill_in.reshape(groups * SLOTS, width), "local", tiled=True)

    main_w, spill_w = pl.pallas_call(
        functools.partial(weight_kernel, groups, experts),
        in_specs=[whole(), whole()],
        out_specs=[whole(), whole()],
        out_shape=[
            jax.ShapeDtypeStruct((experts * SLOTS, tokens), BF16),
            jax.ShapeDtypeStruct((groups * SLOTS, tokens), BF16),
        ],
        compiler_params=params(),
        name="combine_weights",
    )(id_rows, gate_rows)

    main = pl.pallas_call(
        functools.partial(gather_kernel, groups, per_group),
        grid=(per_group,),
        in_specs=[
            scalar(),
            pl.BlockSpec((top, tokens), lambda i: (i, 0)),
            pl.BlockSpec((tokens, width), lambda i: (i, 0)),
        ],
        out_specs=pl.BlockSpec((groups, 1, SLOTS, width), lambda i: (0, i, 0, 0)),
        out_shape=jax.ShapeDtypeStruct((groups, per_group, SLOTS, width), BF16),
        compiler_params=params(),
        name="main_rows",
    )(my_local.reshape(1), ids_all, acts_all)
    main_in = lax.all_to_all(
        main.reshape(groups, per_group * SLOTS, width), "node", split_axis=0, concat_axis=0, tiled=True
    )

    busiest = (jnp.sum((expert_ids == my_expert).astype(jnp.int32)) > SLOTS).astype(jnp.int32).reshape(1)
    spill_out = apply_expert(busiest, spill_all, gate_proj, up_proj, down_proj)
    spill_back = lax.psum_scatter(spill_out, "local", tiled=True)

    always = jnp.ones((1,), jnp.int32)
    main_out = apply_expert(always, main_in.reshape(experts * SLOTS, width), gate_proj, up_proj, down_proj)
    main_back = lax.all_to_all(
        main_out.reshape(experts, SLOTS, width), ("node", "local"), split_axis=0, concat_axis=0, tiled=True
    )
    spill_home = lax.all_to_all(
        spill_back.reshape(groups, SLOTS, width), "node", split_axis=0, concat_axis=0, tiled=True
    )

    columns = min(512, width)
    return pl.pallas_call(
        combine_kernel,
        grid=(width // columns,),
        in_specs=[
            pl.BlockSpec((experts * SLOTS, tokens), lambda i: (0, 0)),
            pl.BlockSpec((groups * SLOTS, tokens), lambda i: (0, 0)),
            pl.BlockSpec((experts * SLOTS, columns), lambda i: (0, i)),
            pl.BlockSpec((groups * SLOTS, columns), lambda i: (0, i)),
        ],
        out_specs=pl.BlockSpec((tokens, columns), lambda i: (0, i)),
        out_shape=jax.ShapeDtypeStruct((tokens, width), BF16),
        compiler_params=params(),
        name="combine",
    )(main_w, spill_w, main_back.reshape(experts * SLOTS, width), spill_home.reshape(groups * SLOTS, width))


def solution(mesh):
    rows = P(("node", "local"), None)
    stacks = P(("node", "local"), None, None)
    return jax.shard_map(
        shards, mesh=mesh, in_specs=(rows, rows, rows, stacks, stacks, stacks), out_specs=rows, check_vma=False
    )
```

```python
import functools

import jax
import jax.numpy as jnp
from jax import lax
from jax.experimental import pallas as pl
from jax.experimental.pallas import tpu as pltpu
from jax.sharding import PartitionSpec as P

SLOTS = 8
SHIFT = 3
BF16 = jnp.bfloat16
F32 = jnp.float32


def iota(shape, dim):
    return lax.broadcasted_iota(jnp.int32, shape, dim)


def indicator(mask):
    return jnp.where(mask, 1.0, 0.0).astype(F32)


def dot(left, right):
    return jnp.dot(left, right, preferred_element_type=F32)


def ranks_of(named):
    tokens = named.shape[1]
    earlier = indicator(iota((tokens, tokens), 0) < iota((tokens, tokens), 1))
    return dot(named.astype(BF16), earlier.astype(BF16))


def spread(values, slots):
    labels = values.shape[0]
    picks = indicator((iota((labels * slots, labels), 0) >> SHIFT) == iota((labels * slots, labels), 1))
    return dot(picks.astype(BF16), values.astype(BF16))


def group_sums(values, groups):
    experts = values.shape[0]
    per_group = experts // groups
    shape = (groups * SLOTS, experts)
    same = indicator((iota(shape, 0) >> SHIFT) == (iota(shape, 1) // per_group))
    return dot(same.astype(BF16), values.astype(BF16))


def marks_of(ids_ref, labels):
    total = indicator(labels == ids_ref[0:1, :])
    for entry in range(1, ids_ref.shape[0]):
        total = total + indicator(labels == ids_ref[entry : entry + 1, :])
    return total


def spill_codes(named, ranks):
    return named * jnp.maximum(ranks - (SLOTS - 1), 0.0)


def pack_kernel(groups, experts, ids_ref, acts_ref, packed_ref, spill_ref):
    tokens, width = acts_ref.shape
    entries = ids_ref.shape[0]
    packed_ref[:, :width] = acts_ref[...]
    ids = ids_ref[...].astype(F32)
    filler = jnp.zeros((tokens - entries, tokens), F32)
    packed_ref[:, width:] = jnp.concatenate([ids, filler], axis=0).astype(BF16)
    named = marks_of(ids_ref, iota((experts, tokens), 0))
    codes = group_sums(spill_codes(named, ranks_of(named)), groups)
    slot = (iota(codes.shape, 0) & (SLOTS - 1)).astype(F32)
    spill_ref[...] = dot(indicator(codes == slot + 1.0).astype(BF16), acts_ref[...]).astype(BF16)


def weight_kernel(groups, experts, ids_ref, gates_ref, main_ref, spill_ref):
    tokens = ids_ref.shape[1]
    labels = iota((experts, tokens), 0)
    named = marks_of(ids_ref, labels)
    gates = jnp.zeros((experts, tokens), F32)
    for entry in range(ids_ref.shape[0]):
        value = gates_ref[entry : entry + 1, :].astype(F32)
        gates = gates + jnp.where(labels == ids_ref[entry : entry + 1, :], value, 0.0)
    ranks = ranks_of(named)
    rank_rows = spread(jnp.where(named > 0.0, ranks, 99.0), SLOTS)
    gate_rows = spread(gates, SLOTS)
    slot = (iota(rank_rows.shape, 0) & (SLOTS - 1)).astype(F32)
    main_ref[...] = jnp.where(rank_rows == slot, gate_rows, 0.0).astype(BF16)
    codes = spill_codes(named, ranks)
    code_rows = group_sums(codes, groups)
    spill_rows = group_sums(jnp.where(codes > 0.0, gates, 0.0), groups)
    spill_slot = (iota(code_rows.shape, 0) & (SLOTS - 1)).astype(F32)
    spill_ref[...] = jnp.where(code_rows == spill_slot + 1.0, spill_rows, 0.0).astype(BF16)


def gather_kernel(groups, per_group, parts, count, my_ref, *refs):
    out_ref = refs[-1]
    width = out_ref.shape[-1]
    mine = my_ref[0]
    core = my_ref[1]
    for place in range(count // parts):
        pieces = refs[place * parts : (place + 1) * parts]
        ids = pieces[0][0:16, width:].astype(F32)[0:8].astype(jnp.int32)
        tokens = ids.shape[1]
        labels = iota((groups, tokens), 0) * per_group + mine
        named = indicator(labels == ids[0:1, :])
        for entry in range(1, ids.shape[0]):
            named = named + indicator(labels == ids[entry : entry + 1, :])
        rank_rows = spread(jnp.where(named > 0.0, ranks_of(named), 99.0), SLOTS)
        slot = (iota(rank_rows.shape, 0) & (SLOTS - 1)).astype(F32)
        picks = indicator(rank_rows == slot).astype(BF16)
        step = tokens // parts
        rows = dot(picks[:, :step], pieces[0][:, :width])
        for part in range(1, parts):
            rows = rows + dot(picks[:, part * step : (part + 1) * step], pieces[part][:, :width])
        rows = rows.reshape(groups, 1, 1, SLOTS, width).astype(BF16)
        side = core if place % 2 == 0 else 1 - core
        out_ref[:, place // 2 : place // 2 + 1, pl.ds(side, 1)] = rows


def expert_rows(blocks, weights, arrive):
    gate_w, up_w, down_w = weights
    arrive(0)
    gates = [dot(rows(), gate_w[...]) for rows in blocks]
    arrive(1)
    ups = [dot(rows(), up_w[...]) for rows in blocks]
    hidden = [(g / (1.0 + jnp.exp(-g)) * u).astype(BF16) for g, u in zip(gates, ups)]
    arrive(2)
    return [dot(rows, down_w[...]).astype(BF16) for rows in hidden]


def weight_copies(sources, weights, sems):
    return [
        pltpu.make_async_copy(source.at[0], weight, sems.at[place])
        for place, (source, weight) in enumerate(zip(sources, weights))
    ]


def main_kernel(first, chips_ref, rows_hbm, gate_hbm, up_hbm, down_hbm, *refs):
    out_hbm, held, done, gate_w, up_w, down_w, row_sems, sems, out_sems = refs[-9:]
    chips, groups, slots, width = held.shape
    weights = (gate_w, up_w, down_w)
    loads = weight_copies((gate_hbm, up_hbm, down_hbm), weights, sems)
    rows = [
        pltpu.make_async_copy(rows_hbm.at[:, chip], held.at[chip], row_sems.at[chip]) for chip in range(chips)
    ]
    for copy in rows + loads:
        copy.start()
    for copy in rows:
        copy.wait()
    blocks = [lambda chip=chip: held[chip].reshape(groups * slots, width) for chip in range(chips)]
    results = expert_rows(blocks, weights, lambda place: loads[place].wait())
    stores = [
        pltpu.make_async_copy(done.at[chip], out_hbm.at[:, chips_ref[first + chip]], out_sems.at[chip])
        for chip in range(chips)
    ]
    for chip in range(chips):
        done[chip] = results[chip].reshape(groups, slots, width)
        stores[chip].start()
    for store in stores:
        store.wait()


def spill_kernel(on_ref, *refs):
    pieces = refs[:10]
    gate_hbm, up_hbm, down_hbm = refs[10:13]
    same_hbm, other_hbm, held, done, gate_w, up_w, down_w, row_sems, sems, out_sems = refs[-10:]
    chips, both, width = held.shape
    tokens = both // 2
    half = tokens // 2
    weights = (gate_w, up_w, down_w)
    places = [(chip, side * tokens, tokens) for chip in range(chips - 1) for side in range(2)]
    places += [(chips - 1, quarter * half, half) for quarter in range(4)]
    loads = weight_copies((gate_hbm, up_hbm, down_hbm), weights, sems)
    rows = [
        pltpu.make_async_copy(piece, held.at[chip, pl.ds(start, count)], row_sems.at[place])
        for place, (piece, (chip, start, count)) in enumerate(zip(pieces, places))
    ]
    stores = [
        pltpu.make_async_copy(done.at[chip, pl.ds(side * tokens, tokens)], out.at[chip], out_sems.at[chip, side])
        for chip in range(chips)
        for side, out in enumerate((same_hbm, other_hbm))
    ]

    @pl.when(on_ref[0] != 0)
    def _():
        for copy in rows + loads:
            copy.start()
        for copy in rows:
            copy.wait()
        for pair in range(chips // 2):
            blocks = [lambda chip=chip: held[chip] for chip in (2 * pair, 2 * pair + 1)]
            results = expert_rows(blocks, weights, lambda place: loads[place].wait() if pair == 0 else None)
            for chip, result in zip((2 * pair, 2 * pair + 1), results):
                done[chip] = result
                stores[2 * chip].start()
                stores[2 * chip + 1].start()

    @pl.when(on_ref[0] == 0)
    def _():
        done[...] = jnp.zeros(done.shape, BF16)
        for store in stores:
            store.start()

    for store in stores:
        store.wait()


def combine_kernel(main_w_ref, spill_w_ref, main_ref, spill_ref, out_ref):
    over_rows = (((0,), (0,)), ((), ()))
    total = lax.dot_general(main_w_ref[...], main_ref[...], over_rows, preferred_element_type=F32)
    total += lax.dot_general(spill_w_ref[...], spill_ref[...], over_rows, preferred_element_type=F32)
    out_ref[...] = total.astype(BF16)


def params(megabytes=48):
    return pltpu.CompilerParams(vmem_limit_bytes=megabytes * 1024 * 1024)


def whole():
    return pl.BlockSpec(memory_space=pltpu.VMEM)


def scalar():
    return pl.BlockSpec(memory_space=pltpu.SMEM)


def anywhere():
    return pl.BlockSpec(memory_space=pl.ANY)


def expert_cost(count, width, hidden):
    return pl.CostEstimate(
        flops=6 * count * width * hidden,
        bytes_accessed=4 * count * width + 6 * width * hidden,
        transcendentals=count * hidden,
    )


def swap_cores(value):
    size = lax.axis_size("local")
    return lax.ppermute(value, "local", [(i, i ^ 1) for i in range(size)])


def next_chip(value, hops):
    size = lax.axis_size("local")
    return lax.ppermute(value, "local", [(i, (i + 2 * hops) % size) for i in range(size)])


def around(value):
    half = value.shape[0] // 2
    before = next_chip(value, 1)
    after = next_chip(value, -1)
    beside = swap_cores(value)
    far_top = next_chip(before[:half], 1)
    far_low = next_chip(after[half:], -1)
    before_beside = swap_cores(before)
    after_beside = swap_cores(after)
    far = [far_top, far_low, swap_cores(far_top), swap_cores(far_low)]
    return [value, beside], [before, before_beside, after, after_beside], far


def order_kernel(value_ref, *refs):
    pass


def after(value, *earlier):
    return pl.pallas_call(
        order_kernel,
        in_specs=[anywhere()] * (1 + len(earlier)),
        out_specs=anywhere(),
        out_shape=jax.ShapeDtypeStruct(value.shape, value.dtype),
        input_output_aliases={0: 0},
        compiler_params=params(60),
        name="order",
    )(value, *earlier)


def back_home(same, other):
    half = same.shape[1] // 2
    total = same + swap_cores(other)
    far = total[3]
    from_before = next_chip(far[:half], 1)
    from_after = next_chip(far[half:], -1)
    to_after = jnp.concatenate([total[2][:half] + from_before, total[2][half:]], axis=0)
    to_before = jnp.concatenate([total[1][:half], total[1][half:] + from_after], axis=0)
    return total[0] + next_chip(to_after, 1) + next_chip(to_before, -1)


def shards(activations, expert_ids, route_gates, gate_proj, up_proj, down_proj):
    tokens, width = activations.shape
    hidden = gate_proj.shape[2]
    groups = lax.axis_size("node")
    per_group = lax.axis_size("local")
    experts = groups * per_group
    chips = per_group // 2
    my_local = lax.axis_index("local").astype(jnp.int32)
    my_expert = lax.axis_index("node").astype(jnp.int32) * per_group + my_local
    my_chip = my_local >> 1
    place = jnp.stack([my_local, my_local & 1])
    order = jnp.stack([my_chip, (my_chip + 3) % chips, (my_chip + 1) % chips, (my_chip + 2) % chips])
    id_rows = expert_ids.T
    gate_rows = route_gates.T

    packed, spill = pl.pallas_call(
        functools.partial(pack_kernel, groups, experts),
        in_specs=[whole(), whole()],
        out_specs=[whole(), whole()],
        out_shape=[
            jax.ShapeDtypeStruct((tokens, width + tokens), BF16),
            jax.ShapeDtypeStruct((groups * SLOTS, width), BF16),
        ],
        compiler_params=params(16),
        name="pack_rows",
    )(id_rows, activations)
    spill_in = lax.all_to_all(spill.reshape(groups, SLOTS, width), "node", split_axis=0, concat_axis=0, tiled=True)

    def pick(pieces, parts):
        return pl.pallas_call(
            functools.partial(gather_kernel, groups, per_group, parts, len(pieces)),
            in_specs=[scalar()] + [whole()] * len(pieces),
            out_specs=whole(),
            out_shape=jax.ShapeDtypeStruct((groups, len(pieces) // parts // 2, 2, SLOTS, width), BF16),
            compiler_params=params(24),
            name="main_rows",
        )(place, *pieces)

    def send(rows):
        count = rows.shape[1]
        sent = rows.reshape(groups, count * 2 * SLOTS, width)
        sent = lax.all_to_all(sent, "node", split_axis=0, concat_axis=0, tiled=True)
        return sent.reshape(groups, count, 2 * SLOTS, width)

    own, near, far = around(packed)
    spill_own, spill_near, spill_far = around(spill_in.reshape(groups * SLOTS, width))
    own_in = send(after(pick(own, 1), spill_in))
    near_rows = pick(near, 1)
    near_in = send(after(near_rows, own_in, spill_near[0], spill_near[2]))
    far_rows = pick(far, 2)

    busiest = (jnp.sum((expert_ids == my_expert).astype(jnp.int32)) > SLOTS).astype(jnp.int32).reshape(1)
    weight_space = [
        pltpu.VMEM((width, hidden), BF16),
        pltpu.VMEM((width, hidden), BF16),
        pltpu.VMEM((hidden, width), BF16),
    ]
    earlier = [own_in]
    spill_same, spill_other = pl.pallas_call(
        spill_kernel,
        in_specs=[scalar()] + [anywhere()] * (13 + len(earlier)),
        out_specs=[anywhere(), anywhere()],
        out_shape=[jax.ShapeDtypeStruct((chips, groups * SLOTS, width), BF16)] * 2,
        scratch_shapes=[pltpu.VMEM((chips, 2 * groups * SLOTS, width), BF16)] * 2
        + weight_space
        + [pltpu.SemaphoreType.DMA((10,)), pltpu.SemaphoreType.DMA((3,)), pltpu.SemaphoreType.DMA((chips, 2))],
        compiler_params=params(60),
        cost_estimate=expert_cost(per_group * groups * SLOTS, width, hidden),
        name="spill_expert",
    )(busiest, *spill_own, *spill_near, *spill_far, gate_proj, up_proj, down_proj, *earlier)
    far_in = send(after(far_rows, near_in, spill_same))
    spill_back = back_home(spill_same, after(spill_other, near_in))

    main_out = spill_same
    first = 0
    for arrival in (own_in, near_in, far_in):
        count = arrival.shape[1]
        main_out = pl.pallas_call(
            functools.partial(main_kernel, first),
            in_specs=[scalar()] + [anywhere()] * 5,
            out_specs=anywhere(),
            out_shape=jax.ShapeDtypeStruct((groups, chips, 2 * SLOTS, width), BF16),
            scratch_shapes=[pltpu.VMEM((count, groups, 2 * SLOTS, width), BF16)] * 2
            + weight_space
            + [pltpu.SemaphoreType.DMA((count,)), pltpu.SemaphoreType.DMA((3,)), pltpu.SemaphoreType.DMA((count,))],
            input_output_aliases={5: 0} if first else {},
            compiler_params=params(60),
            cost_estimate=expert_cost(count * 2 * groups * SLOTS, width, hidden),
            name="main_expert",
        )(order, arrival, gate_proj, up_proj, down_proj, main_out)
        first += count

    main_w, spill_w = pl.pallas_call(
        functools.partial(weight_kernel, groups, experts),
        in_specs=[whole(), whole()],
        out_specs=[whole(), whole()],
        out_shape=[
            jax.ShapeDtypeStruct((experts * SLOTS, tokens), BF16),
            jax.ShapeDtypeStruct((groups * SLOTS, tokens), BF16),
        ],
        compiler_params=params(16),
        name="combine_weights",
    )(id_rows, gate_rows)
    main_back = lax.all_to_all(
        main_out.reshape(experts, SLOTS, width), ("node", "local"), split_axis=0, concat_axis=0, tiled=True
    )
    spill_home = lax.all_to_all(
        after(spill_back, main_back).reshape(groups, SLOTS, width), "node", split_axis=0, concat_axis=0, tiled=True
    )

    columns = min(1024, width)
    return pl.pallas_call(
        combine_kernel,
        grid=(width // columns,),
        in_specs=[
            pl.BlockSpec((experts * SLOTS, tokens), lambda i: (0, 0)),
            pl.BlockSpec((groups * SLOTS, tokens), lambda i: (0, 0)),
            pl.BlockSpec((experts * SLOTS, columns), lambda i: (0, i)),
            pl.BlockSpec((groups * SLOTS, columns), lambda i: (0, i)),
        ],
        out_specs=pl.BlockSpec((tokens, columns), lambda i: (0, i)),
        out_shape=jax.ShapeDtypeStruct((tokens, width), BF16),
        compiler_params=params(60),
        name="combine",
    )(main_w, spill_w, main_back.reshape(experts * SLOTS, width), spill_home.reshape(groups * SLOTS, width))


def solution(mesh):
    rows = P(("node", "local"), None)
    stacks = P(("node", "local"), None, None)
    return jax.shard_map(
        shards, mesh=mesh, in_specs=(rows, rows, rows, stacks, stacks, stacks), out_specs=rows, check_vma=False
    )
```

```python
import functools

import jax
import jax.numpy as jnp
from jax import lax
from jax.experimental import pallas as pl
from jax.experimental.pallas import tpu as pltpu
from jax.sharding import PartitionSpec as P

SLOTS = 8
SHIFT = 3
BF16 = jnp.bfloat16
F32 = jnp.float32


def iota(shape, dim):
    return lax.broadcasted_iota(jnp.int32, shape, dim)


def indicator(mask):
    return jnp.where(mask, 1.0, 0.0).astype(F32)


def dot(left, right):
    return jnp.dot(left, right, preferred_element_type=F32)


def ranks_of(named):
    tokens = named.shape[1]
    earlier = indicator(iota((tokens, tokens), 0) < iota((tokens, tokens), 1))
    return dot(named.astype(BF16), earlier.astype(BF16))


def spread(values, slots):
    labels = values.shape[0]
    picks = indicator((iota((labels * slots, labels), 0) >> SHIFT) == iota((labels * slots, labels), 1))
    return dot(picks.astype(BF16), values.astype(BF16))


def group_sums(values, groups):
    experts = values.shape[0]
    per_group = experts // groups
    shape = (groups * SLOTS, experts)
    same = indicator((iota(shape, 0) >> SHIFT) == (iota(shape, 1) // per_group))
    return dot(same.astype(BF16), values.astype(BF16))


def marks_of(ids_ref, labels):
    total = indicator(labels == ids_ref[0:1, :])
    for entry in range(1, ids_ref.shape[0]):
        total = total + indicator(labels == ids_ref[entry : entry + 1, :])
    return total


def spill_codes(named, ranks):
    return named * jnp.maximum(ranks - (SLOTS - 1), 0.0)


def pack_kernel(ids_ref, acts_ref, packed_ref):
    tokens, width = acts_ref.shape
    entries = ids_ref.shape[0]
    packed_ref[:, :width] = acts_ref[...]
    ids = ids_ref[...].astype(F32)
    filler = jnp.zeros((tokens - entries, tokens), F32)
    packed_ref[:, width:] = jnp.concatenate([ids, filler], axis=0).astype(BF16)


def weight_kernel(groups, experts, ids_ref, gates_ref, main_ref, spill_ref):
    tokens = ids_ref.shape[1]
    labels = iota((experts, tokens), 0)
    named = marks_of(ids_ref, labels)
    gates = jnp.zeros((experts, tokens), F32)
    for entry in range(ids_ref.shape[0]):
        value = gates_ref[entry : entry + 1, :].astype(F32)
        gates = gates + jnp.where(labels == ids_ref[entry : entry + 1, :], value, 0.0)
    ranks = ranks_of(named)
    rank_rows = spread(jnp.where(named > 0.0, ranks, 99.0), SLOTS)
    gate_rows = spread(gates, SLOTS)
    slot = (iota(rank_rows.shape, 0) & (SLOTS - 1)).astype(F32)
    main_ref[...] = jnp.where(rank_rows == slot, gate_rows, 0.0).astype(BF16)
    codes = spill_codes(named, ranks)
    code_rows = group_sums(codes, groups)
    spill_rows = group_sums(jnp.where(codes > 0.0, gates, 0.0), groups)
    spill_slot = (iota(code_rows.shape, 0) & (SLOTS - 1)).astype(F32)
    spill_ref[...] = jnp.where(code_rows == spill_slot + 1.0, spill_rows, 0.0).astype(BF16)


def ids_of(packed_ref, width):
    return packed_ref[0:16, width:].astype(F32)[0:8].astype(jnp.int32)


def picks_for(ids, groups, per_group, mine):
    named = marks_of(ids, iota((groups, ids.shape[1]), 0) * per_group + mine)
    rank_rows = spread(jnp.where(named > 0.0, ranks_of(named), 99.0), SLOTS)
    slot = (iota(rank_rows.shape, 0) & (SLOTS - 1)).astype(F32)
    return indicator(rank_rows == slot).astype(BF16)


def gather_kernel(groups, per_group, parts, with_spill, my_ref, *refs):
    out_hbm, held, sem = refs[-3:]
    pieces = refs[:-3]
    width = held.shape[-1]
    core = my_ref[1]
    for place in range(len(pieces) // parts):
        block = pieces[place * parts : (place + 1) * parts]
        picks = picks_for(ids_of(block[0], width), groups, per_group, my_ref[0])
        step = picks.shape[1] // parts
        rows = dot(picks[:, :step], block[0][:, :width])
        for part in range(1, parts):
            rows = rows + dot(picks[:, part * step : (part + 1) * step], block[part][:, :width])
        side = core if place % 2 == 0 else 1 - core
        held[:, pl.ds(2 * (place // 2) + side, 1)] = rows.reshape(groups, 1, SLOTS, width).astype(BF16)
    if with_spill:
        ids = ids_of(pieces[0], width)
        named = marks_of(ids, iota((groups * per_group, ids.shape[1]), 0))
        codes = group_sums(spill_codes(named, ranks_of(named)), groups)
        slot = (iota(codes.shape, 0) & (SLOTS - 1)).astype(F32)
        rows = dot(indicator(codes == slot + 1.0).astype(BF16), pieces[0][:, :width])
        held[:, held.shape[1] - 1] = rows.reshape(groups, SLOTS, width).astype(BF16)
    copy = pltpu.make_async_copy(held, out_hbm, sem)
    copy.start()
    copy.wait()


SLICES = 3


def expert_loads(sources, weights, sems):
    gate_hbm, up_hbm, down_hbm = sources
    gate_w, up_w, down_w = weights
    step = gate_w.shape[2]
    loads = []
    for part in range(SLICES):
        units = pl.ds(part * step, step)
        loads.append(
            (
                pltpu.make_async_copy(gate_hbm.at[0, :, units], gate_w.at[part], sems.at[part, 0]),
                pltpu.make_async_copy(up_hbm.at[0, :, units], up_w.at[part], sems.at[part, 1]),
                pltpu.make_async_copy(down_hbm.at[0, units], down_w.at[part], sems.at[part, 2]),
            )
        )
    return loads


def expert_rows(blocks, weights, loads, fresh=True):
    gate_w, up_w, down_w = weights
    totals = [None] * len(blocks)
    for part in range(SLICES):
        if fresh:
            loads[part][0].wait()
            loads[part][2].start()
            if part + 1 < SLICES:
                loads[part + 1][0].start()
                loads[part + 1][1].start()
        gates = [dot(rows(), gate_w[part]) for rows in blocks]
        if fresh:
            loads[part][1].wait()
        ups = [dot(rows(), up_w[part]) for rows in blocks]
        hidden = [(g / (1.0 + jnp.exp(-g)) * u).astype(BF16) for g, u in zip(gates, ups)]
        if fresh:
            loads[part][2].wait()
        outs = [dot(rows, down_w[part]) for rows in hidden]
        totals = [out if total is None else total + out for total, out in zip(totals, outs)]
    return [total.astype(BF16) for total in totals]


def main_kernel(first, chips_ref, rows_hbm, gate_hbm, up_hbm, down_hbm, *refs):
    out_hbm, held, done, gate_w, up_w, down_w, row_sems, sems, out_sems = refs[-9:]
    chips, groups, slots, width = held.shape
    weights = (gate_w, up_w, down_w)
    loads = expert_loads((gate_hbm, up_hbm, down_hbm), weights, sems)
    rows = [
        pltpu.make_async_copy(rows_hbm.at[:, pl.ds(chip * slots, slots)], held.at[chip], row_sems.at[chip])
        for chip in range(chips)
    ]
    for copy in [*rows, loads[0][0], loads[0][1]]:
        copy.start()
    for copy in rows:
        copy.wait()
    blocks = [lambda chip=chip: held[chip].reshape(groups * slots, width) for chip in range(chips)]
    results = expert_rows(blocks, weights, loads)
    stores = [
        pltpu.make_async_copy(done.at[chip], out_hbm.at[:, chips_ref[first + chip]], out_sems.at[chip])
        for chip in range(chips)
    ]
    for chip in range(chips):
        done[chip] = results[chip].reshape(groups, slots, width)
        stores[chip].start()
    for store in stores:
        store.wait()


def spill_kernel(on_ref, *refs):
    pieces = refs[:10]
    gate_hbm, up_hbm, down_hbm = refs[10:13]
    same_hbm, other_hbm, held, done, gate_w, up_w, down_w, row_sems, sems, out_sems = refs[-10:]
    chips, both, width = held.shape
    tokens = both // 2
    half = tokens // 2
    weights = (gate_w, up_w, down_w)
    places = [(chip, side * tokens, tokens) for chip in range(chips - 1) for side in range(2)]
    places += [(chips - 1, quarter * half, half) for quarter in range(4)]
    loads = expert_loads((gate_hbm, up_hbm, down_hbm), weights, sems)
    rows = [
        pltpu.make_async_copy(piece, held.at[chip, pl.ds(start, count)], row_sems.at[place])
        for place, (piece, (chip, start, count)) in enumerate(zip(pieces, places))
    ]
    stores = [
        pltpu.make_async_copy(done.at[chip, pl.ds(side * tokens, tokens)], out.at[chip], out_sems.at[chip, side])
        for chip in range(chips)
        for side, out in enumerate((same_hbm, other_hbm))
    ]

    @pl.when(on_ref[0] != 0)
    def _():
        for copy in [*rows, loads[0][0], loads[0][1]]:
            copy.start()
        for copy in rows:
            copy.wait()
        for pair in range(chips // 2):
            blocks = [lambda chip=chip: held[chip] for chip in (2 * pair, 2 * pair + 1)]
            results = expert_rows(blocks, weights, loads, pair == 0)
            for chip, result in zip((2 * pair, 2 * pair + 1), results):
                done[chip] = result
                stores[2 * chip].start()
                stores[2 * chip + 1].start()

    @pl.when(on_ref[0] == 0)
    def _():
        done[...] = jnp.zeros(done.shape, BF16)
        for store in stores:
            store.start()

    for store in stores:
        store.wait()


def combine_kernel(main_w_ref, spill_w_ref, main_ref, spill_ref, out_ref):
    over_rows = (((0,), (0,)), ((), ()))
    total = lax.dot_general(main_w_ref[...], main_ref[...], over_rows, preferred_element_type=F32)
    total += lax.dot_general(spill_w_ref[...], spill_ref[...], over_rows, preferred_element_type=F32)
    out_ref[...] = total.astype(BF16)


def params(megabytes=48):
    return pltpu.CompilerParams(vmem_limit_bytes=megabytes * 1024 * 1024)


def whole():
    return pl.BlockSpec(memory_space=pltpu.VMEM)


def scalar():
    return pl.BlockSpec(memory_space=pltpu.SMEM)


def hbm():
    return pl.BlockSpec(memory_space=pltpu.HBM)


def anywhere():
    return pl.BlockSpec(memory_space=pl.ANY)


def expert_cost(count, width, hidden):
    return pl.CostEstimate(
        flops=6 * count * width * hidden,
        bytes_accessed=4 * count * width + 6 * width * hidden,
        transcendentals=count * hidden,
    )


def swap_cores(value):
    size = lax.axis_size("local")
    return lax.ppermute(value, "local", [(i, i ^ 1) for i in range(size)])


def next_chip(value, hops):
    size = lax.axis_size("local")
    return lax.ppermute(value, "local", [(i, (i + 2 * hops) % size) for i in range(size)])


def around(value):
    half = value.shape[0] // 2
    before = next_chip(value, 1)
    after = next_chip(value, -1)
    beside = swap_cores(value)
    far_top = next_chip(before[:half], 1)
    far_low = next_chip(after[half:], -1)
    before_beside = swap_cores(before)
    after_beside = swap_cores(after)
    far = [far_top, far_low, swap_cores(far_top), swap_cores(far_low)]
    return [value, beside], [before, before_beside, after, after_beside], far


def order_kernel(value_ref, *refs):
    pass


def after(value, *earlier):
    return pl.pallas_call(
        order_kernel,
        in_specs=[hbm()] + [anywhere()] * len(earlier),
        out_specs=hbm(),
        out_shape=jax.ShapeDtypeStruct(value.shape, value.dtype),
        input_output_aliases={0: 0},
        compiler_params=params(60),
        name="order",
    )(value, *earlier)


def shards(activations, expert_ids, route_gates, gate_proj, up_proj, down_proj):
    tokens, width = activations.shape
    hidden = gate_proj.shape[2]
    groups = lax.axis_size("node")
    per_group = lax.axis_size("local")
    experts = groups * per_group
    chips = per_group // 2
    my_local = lax.axis_index("local").astype(jnp.int32)
    my_expert = lax.axis_index("node").astype(jnp.int32) * per_group + my_local
    my_chip = my_local >> 1
    place = jnp.stack([my_local, my_local & 1])
    order = jnp.stack([my_chip, (my_chip + 3) % chips, (my_chip + 1) % chips, (my_chip + 2) % chips])
    id_rows = expert_ids.T
    gate_rows = route_gates.T

    packed = pl.pallas_call(
        pack_kernel,
        in_specs=[whole(), whole()],
        out_specs=whole(),
        out_shape=jax.ShapeDtypeStruct((tokens, width + tokens), BF16),
        compiler_params=params(16),
        name="pack_rows",
    )(id_rows, activations)

    def pick(pieces, parts, with_spill):
        count = len(pieces) // parts + with_spill
        return pl.pallas_call(
            functools.partial(gather_kernel, groups, per_group, parts, with_spill),
            in_specs=[scalar()] + [whole()] * len(pieces),
            out_specs=hbm(),
            out_shape=jax.ShapeDtypeStruct((groups, count, SLOTS, width), BF16),
            scratch_shapes=[pltpu.VMEM((groups, count, SLOTS, width), BF16), pltpu.SemaphoreType.DMA],
            compiler_params=params(24),
            name="main_rows",
        )(place, *pieces)

    def send(rows):
        sent = rows.reshape(groups, rows.shape[1] * SLOTS, width)
        return lax.all_to_all(sent, "node", split_axis=0, concat_axis=0, tiled=True)

    own, near, far = around(packed)
    own_in = send(pick(own, 1, True))
    near_rows = pick(near, 1, False)
    near_in = send(after(near_rows, own_in))
    spill_in = own_in[:, 2 * SLOTS :].reshape(groups * SLOTS, width)
    spill_own, spill_near, spill_far = around(spill_in)

    busiest = (jnp.sum((expert_ids == my_expert).astype(jnp.int32)) > SLOTS).astype(jnp.int32).reshape(1)
    step = hidden // SLICES
    weight_space = [
        pltpu.VMEM((SLICES, width, step), BF16),
        pltpu.VMEM((SLICES, width, step), BF16),
        pltpu.VMEM((SLICES, step, width), BF16),
    ]
    spill_same, spill_other = pl.pallas_call(
        spill_kernel,
        in_specs=[scalar()] + [anywhere()] * 15,
        out_specs=[hbm(), hbm()],
        out_shape=[jax.ShapeDtypeStruct((chips, groups * SLOTS, width), BF16)] * 2,
        scratch_shapes=[pltpu.VMEM((chips, 2 * groups * SLOTS, width), BF16)] * 2
        + weight_space
        + [pltpu.SemaphoreType.DMA((10,)), pltpu.SemaphoreType.DMA((SLICES, 3)), pltpu.SemaphoreType.DMA((chips, 2))],
        compiler_params=params(60),
        cost_estimate=expert_cost(per_group * groups * SLOTS, width, hidden),
        name="spill_expert",
    )(busiest, *spill_own, *spill_near, *spill_far, gate_proj, up_proj, down_proj, far[2], far[3])
    far_in = send(after(pick(far, 2, False), near_in, spill_same))

    def main_expert(arrival, first, count, main_out, *earlier):
        return pl.pallas_call(
            functools.partial(main_kernel, first),
            in_specs=[scalar()] + [anywhere()] * (5 + len(earlier)),
            out_specs=hbm(),
            out_shape=jax.ShapeDtypeStruct((groups, chips, 2 * SLOTS, width), BF16),
            scratch_shapes=[pltpu.VMEM((count, groups, 2 * SLOTS, width), BF16)] * 2
            + weight_space
            + [pltpu.SemaphoreType.DMA((count,)), pltpu.SemaphoreType.DMA((SLICES, 3)), pltpu.SemaphoreType.DMA((count,))],
            input_output_aliases={5: 0} if first else {},
            compiler_params=params(60),
            cost_estimate=expert_cost(count * 2 * groups * SLOTS, width, hidden),
            name="main_expert",
        )(order, arrival, gate_proj, up_proj, down_proj, main_out, *earlier)

    main_out = main_expert(own_in, 0, 1, spill_same, near_in)
    half = groups * SLOTS // 2
    total = spill_same + swap_cores(after(spill_other, near_in))
    from_before = next_chip(total[3, :half], 1)
    from_after = next_chip(total[3, half:], -1)
    main_out = main_expert(near_in, 1, 2, main_out, total)
    to_after = jnp.concatenate([total[2, :half] + from_before, total[2, half:]], axis=0)
    to_before = jnp.concatenate([total[1, :half], total[1, half:] + from_after], axis=0)
    main_out = main_expert(far_in, 3, 1, main_out, to_after, to_before)
    spill_back = total[0] + next_chip(to_after, 1) + next_chip(to_before, -1)

    main_w, spill_w = pl.pallas_call(
        functools.partial(weight_kernel, groups, experts),
        in_specs=[whole(), whole()],
        out_specs=[whole(), whole()],
        out_shape=[
            jax.ShapeDtypeStruct((experts * SLOTS, tokens), BF16),
            jax.ShapeDtypeStruct((groups * SLOTS, tokens), BF16),
        ],
        compiler_params=params(16),
        name="combine_weights",
    )(id_rows, gate_rows)
    main_back = lax.all_to_all(
        main_out.reshape(experts, SLOTS, width), ("node", "local"), split_axis=0, concat_axis=0, tiled=True
    )
    spill_home = lax.all_to_all(
        after(spill_back, main_back).reshape(groups, SLOTS, width), "node", split_axis=0, concat_axis=0, tiled=True
    )

    columns = min(1024, width)
    return pl.pallas_call(
        combine_kernel,
        grid=(width // columns,),
        in_specs=[
            pl.BlockSpec((experts * SLOTS, tokens), lambda i: (0, 0)),
            pl.BlockSpec((groups * SLOTS, tokens), lambda i: (0, 0)),
            pl.BlockSpec((experts * SLOTS, columns), lambda i: (0, i)),
            pl.BlockSpec((groups * SLOTS, columns), lambda i: (0, i)),
        ],
        out_specs=pl.BlockSpec((tokens, columns), lambda i: (0, i)),
        out_shape=jax.ShapeDtypeStruct((tokens, width), BF16),
        compiler_params=params(60),
        name="combine",
    )(main_w, spill_w, main_back.reshape(experts * SLOTS, width), spill_home.reshape(groups * SLOTS, width))


def solution(mesh):
    rows = P(("node", "local"), None)
    stacks = P(("node", "local"), None, None)
    return jax.shard_map(
        shards, mesh=mesh, in_specs=(rows, rows, rows, stacks, stacks, stacks), out_specs=rows, check_vma=False
    )
```

```python
import functools

import jax
import jax.numpy as jnp
from jax import lax
from jax.experimental import pallas as pl
from jax.experimental.pallas import tpu as pltpu
from jax.sharding import PartitionSpec as P

SLOTS = 8
SHIFT = 3
BF16 = jnp.bfloat16
F32 = jnp.float32


def iota(shape, dim):
    return lax.broadcasted_iota(jnp.int32, shape, dim)


def indicator(mask):
    return jnp.where(mask, 1.0, 0.0).astype(F32)


def dot(left, right):
    return jnp.dot(left, right, preferred_element_type=F32)


def ranks_of(named):
    tokens = named.shape[1]
    earlier = indicator(iota((tokens, tokens), 0) < iota((tokens, tokens), 1))
    return dot(named.astype(BF16), earlier.astype(BF16))


def spread(values, slots):
    labels = values.shape[0]
    picks = indicator((iota((labels * slots, labels), 0) >> SHIFT) == iota((labels * slots, labels), 1))
    return dot(picks.astype(BF16), values.astype(BF16))


def group_sums(values, groups):
    experts = values.shape[0]
    per_group = experts // groups
    shape = (groups * SLOTS, experts)
    same = indicator((iota(shape, 0) >> SHIFT) == (iota(shape, 1) // per_group))
    return dot(same.astype(BF16), values.astype(BF16))


def marks_of(ids_ref, labels):
    total = indicator(labels == ids_ref[0:1, :])
    for entry in range(1, ids_ref.shape[0]):
        total = total + indicator(labels == ids_ref[entry : entry + 1, :])
    return total


def spill_codes(named, ranks):
    return named * jnp.maximum(ranks - (SLOTS - 1), 0.0)


def pack_kernel(groups, experts, ids_ref, acts_ref, packed_ref, spill_ref):
    tokens, width = acts_ref.shape
    entries = ids_ref.shape[0]
    packed_ref[:, :width] = acts_ref[...]
    ids = ids_ref[...].astype(F32)
    filler = jnp.zeros((tokens - entries, tokens), F32)
    packed_ref[:, width:] = jnp.concatenate([ids, filler], axis=0).astype(BF16)
    named = marks_of(ids_ref, iota((experts, tokens), 0))
    codes = group_sums(spill_codes(named, ranks_of(named)), groups)
    slot = (iota(codes.shape, 0) & (SLOTS - 1)).astype(F32)
    spill_ref[...] = dot(indicator(codes == slot + 1.0).astype(BF16), acts_ref[...]).astype(BF16)


def weight_kernel(groups, experts, ids_ref, gates_ref, main_ref, spill_ref):
    tokens = ids_ref.shape[1]
    labels = iota((experts, tokens), 0)
    named = marks_of(ids_ref, labels)
    gates = jnp.zeros((experts, tokens), F32)
    for entry in range(ids_ref.shape[0]):
        value = gates_ref[entry : entry + 1, :].astype(F32)
        gates = gates + jnp.where(labels == ids_ref[entry : entry + 1, :], value, 0.0)
    ranks = ranks_of(named)
    rank_rows = spread(jnp.where(named > 0.0, ranks, 99.0), SLOTS)
    gate_rows = spread(gates, SLOTS)
    slot = (iota(rank_rows.shape, 0) & (SLOTS - 1)).astype(F32)
    main_ref[...] = jnp.where(rank_rows == slot, gate_rows, 0.0).astype(BF16)
    codes = spill_codes(named, ranks)
    code_rows = group_sums(codes, groups)
    spill_rows = group_sums(jnp.where(codes > 0.0, gates, 0.0), groups)
    spill_slot = (iota(code_rows.shape, 0) & (SLOTS - 1)).astype(F32)
    spill_ref[...] = jnp.where(code_rows == spill_slot + 1.0, spill_rows, 0.0).astype(BF16)


def picks_for(ids, groups, per_group, mine):
    named = marks_of(ids, iota((groups, ids.shape[1]), 0) * per_group + mine)
    rank_rows = spread(jnp.where(named > 0.0, ranks_of(named), 99.0), SLOTS)
    slot = (iota(rank_rows.shape, 0) & (SLOTS - 1)).astype(F32)
    return indicator(rank_rows == slot).astype(BF16)


def gather_kernel(groups, per_group, my_ref, ids_ref, acts_ref, out_ref, picks):
    sources, _, tokens = picks.shape

    @pl.when(pl.program_id(0) == 0)
    def _():
        for source in range(sources):
            ids = ids_ref[source * tokens : source * tokens + 16].astype(F32)[0:8].astype(jnp.int32)
            picks[source] = picks_for(ids, groups, per_group, my_ref[0])

    for source in range(sources):
        rows = dot(picks[source], acts_ref[source * tokens : (source + 1) * tokens])
        out_ref[:, source] = rows.reshape(groups, SLOTS, rows.shape[1]).astype(BF16)


CHUNKS = 4


def expert_loads(sources, weights, sems):
    loads = []
    for place, (source, weight) in enumerate(zip(sources, weights)):
        rows = weight.shape[0] // CHUNKS
        loads.append(
            [
                pltpu.make_async_copy(
                    source.at[0, pl.ds(part * rows, rows)], weight.at[pl.ds(part * rows, rows)], sems.at[place, part]
                )
                for part in range(CHUNKS)
            ]
        )
    return loads


def wait_all(copies):
    for copy in copies:
        copy.wait()


def expert_rows(blocks, weights, loads):
    gate_w, up_w, down_w = weights
    if loads:
        wait_all(loads[0])
    gates = [dot(rows(), gate_w[...]) for rows in blocks]
    if loads:
        wait_all(loads[1])
    ups = [dot(rows(), up_w[...]) for rows in blocks]
    hidden = [(g / (1.0 + jnp.exp(-g)) * u).astype(BF16) for g, u in zip(gates, ups)]
    if loads:
        wait_all(loads[2])
    return [dot(rows, down_w[...]).astype(BF16) for rows in hidden]


def main_kernel(first, rows_hbm, gate_hbm, up_hbm, down_hbm, *refs):
    out_hbm, held, done, gate_w, up_w, down_w, row_sems, sems, out_sems = refs[-9:]
    chips, groups, slots, width = held.shape
    weights = (gate_w, up_w, down_w)
    loads = expert_loads((gate_hbm, up_hbm, down_hbm), weights, sems)
    rows = [
        pltpu.make_async_copy(rows_hbm.at[:, pl.ds(chip * slots, slots)], held.at[chip], row_sems.at[chip])
        for chip in range(chips)
    ]
    for copy in rows + loads[0] + loads[1] + loads[2]:
        copy.start()
    wait_all(rows)
    blocks = [lambda chip=chip: held[chip].reshape(groups * slots, width) for chip in range(chips)]
    results = expert_rows(blocks, weights, loads)
    stores = [
        pltpu.make_async_copy(done.at[chip], out_hbm.at[:, first + chip], out_sems.at[chip]) for chip in range(chips)
    ]
    for chip in range(chips):
        done[chip] = results[chip].reshape(groups, slots, width)
        stores[chip].start()
    wait_all(stores)


def spill_kernel(on_ref, rows_hbm, gate_hbm, up_hbm, down_hbm, *refs):
    out_hbm, held, done, gate_w, up_w, down_w, row_sems, sems, out_sems = refs[-9:]
    blocks, count, _ = held.shape
    weights = (gate_w, up_w, down_w)
    loads = expert_loads((gate_hbm, up_hbm, down_hbm), weights, sems)
    rows = [
        pltpu.make_async_copy(rows_hbm.at[pl.ds(block * count, count)], held.at[block], row_sems.at[block])
        for block in range(blocks)
    ]
    stores = [
        pltpu.make_async_copy(done.at[block], out_hbm.at[pl.ds(block * count, count)], out_sems.at[block])
        for block in range(blocks)
    ]

    @pl.when(on_ref[0] != 0)
    def _():
        for copy in rows + loads[0] + loads[1] + loads[2]:
            copy.start()
        wait_all(rows)
        for pair in range(0, blocks, 2):
            both = [lambda block=block: held[block] for block in (pair, pair + 1)]
            results = expert_rows(both, weights, loads if pair == 0 else None)
            for block, result in zip((pair, pair + 1), results):
                done[block] = result
                stores[block].start()

    @pl.when(on_ref[0] == 0)
    def _():
        done[...] = jnp.zeros(done.shape, BF16)
        for store in stores:
            store.start()

    wait_all(stores)


def combine_kernel(main_w_ref, spill_w_ref, main_ref, spill_ref, out_ref):
    over_rows = (((0,), (0,)), ((), ()))
    total = lax.dot_general(main_w_ref[...], main_ref[...], over_rows, preferred_element_type=F32)
    total += lax.dot_general(spill_w_ref[...], spill_ref[...], over_rows, preferred_element_type=F32)
    out_ref[...] = total.astype(BF16)


def params(megabytes=48):
    return pltpu.CompilerParams(vmem_limit_bytes=megabytes * 1024 * 1024)


def whole():
    return pl.BlockSpec(memory_space=pltpu.VMEM)


def scalar():
    return pl.BlockSpec(memory_space=pltpu.SMEM)


def hbm():
    return pl.BlockSpec(memory_space=pltpu.HBM)


def anywhere():
    return pl.BlockSpec(memory_space=pl.ANY)


def expert_cost(count, width, hidden):
    return pl.CostEstimate(
        flops=6 * count * width * hidden,
        bytes_accessed=4 * count * width + 6 * width * hidden,
        transcendentals=count * hidden,
    )


def order_kernel(value_ref, *refs):
    pass


def after(value, *earlier):
    return pl.pallas_call(
        order_kernel,
        in_specs=[hbm()] + [anywhere()] * len(earlier),
        out_specs=hbm(),
        out_shape=jax.ShapeDtypeStruct(value.shape, value.dtype),
        input_output_aliases={0: 0},
        compiler_params=params(60),
        name="order",
    )(value, *earlier)


def shards(activations, expert_ids, route_gates, gate_proj, up_proj, down_proj):
    tokens, width = activations.shape
    hidden = gate_proj.shape[2]
    groups = lax.axis_size("node")
    per_group = lax.axis_size("local")
    experts = groups * per_group
    chips = per_group // 2
    my_node = lax.axis_index("node").astype(jnp.int32)
    my_local = lax.axis_index("local").astype(jnp.int32)
    my_expert = my_node * per_group + my_local
    id_rows = expert_ids.T
    gate_rows = route_gates.T

    packed, spill = pl.pallas_call(
        functools.partial(pack_kernel, groups, experts),
        in_specs=[whole(), whole()],
        out_specs=[whole(), whole()],
        out_shape=[
            jax.ShapeDtypeStruct((tokens, width + tokens), BF16),
            jax.ShapeDtypeStruct((groups * SLOTS, width), BF16),
        ],
        compiler_params=params(60),
        name="pack_rows",
    )(id_rows, activations)
    packed_all = lax.all_gather(packed, "local", tiled=True)
    spill_in = lax.all_to_all(spill.reshape(groups, SLOTS, width), "node", split_axis=0, concat_axis=0, tiled=True)
    spill_in = after(spill_in.reshape(groups * SLOTS, width), packed_all)
    spill_all = lax.all_gather(spill_in, "local", tiled=True)

    columns = min(1024, width)

    def pick(part, sources):
        return pl.pallas_call(
            functools.partial(gather_kernel, groups, per_group),
            grid=(width // columns,),
            in_specs=[
                scalar(),
                pl.BlockSpec((sources * tokens, tokens), lambda i: (part, width // tokens)),
                pl.BlockSpec((sources * tokens, columns), lambda i: (part, i)),
            ],
            out_specs=pl.BlockSpec((groups, sources, SLOTS, columns), lambda i: (0, 0, 0, i)),
            out_shape=jax.ShapeDtypeStruct((groups, sources, SLOTS, width), BF16),
            scratch_shapes=[pltpu.VMEM((sources, groups * SLOTS, tokens), BF16)],
            compiler_params=params(60),
            name="main_rows",
        )(my_local.reshape(1), packed_all, packed_all)

    def send(rows):
        sent = rows.reshape(groups, rows.shape[1] * SLOTS, width)
        return lax.all_to_all(sent, "node", split_axis=0, concat_axis=0, tiled=True)

    late_chips = 1
    early_chips = chips - late_chips
    early_in = send(pick(0, 2 * early_chips))
    late_rows = pick(early_chips // late_chips, 2 * late_chips)

    weight_space = [
        pltpu.VMEM((width, hidden), BF16),
        pltpu.VMEM((width, hidden), BF16),
        pltpu.VMEM((hidden, width), BF16),
    ]
    busiest = (jnp.sum((expert_ids == my_expert).astype(jnp.int32)) > SLOTS).astype(jnp.int32).reshape(1)
    spill_rows = groups * SLOTS * per_group
    spill_out = pl.pallas_call(
        spill_kernel,
        in_specs=[scalar()] + [anywhere()] * 4,
        out_specs=hbm(),
        out_shape=jax.ShapeDtypeStruct((spill_rows, width), BF16),
        scratch_shapes=[pltpu.VMEM((4, spill_rows // 4, width), BF16)] * 2
        + weight_space
        + [pltpu.SemaphoreType.DMA((4,)), pltpu.SemaphoreType.DMA((3, CHUNKS)), pltpu.SemaphoreType.DMA((4,))],
        compiler_params=params(60),
        cost_estimate=expert_cost(spill_rows, width, hidden),
        name="spill_expert",
    )(busiest, spill_all, gate_proj, up_proj, down_proj)
    spill_out = after(spill_out, early_in)
    late_in = send(after(late_rows, early_in, spill_out))
    spill_back = lax.psum_scatter(spill_out, "local", tiled=True)

    def main_expert(arrival, first, count, *main_out):
        return pl.pallas_call(
            functools.partial(main_kernel, first),
            in_specs=[anywhere()] * (4 + len(main_out)),
            out_specs=hbm(),
            out_shape=jax.ShapeDtypeStruct((groups, chips, 2 * SLOTS, width), BF16),
            scratch_shapes=[pltpu.VMEM((count, groups, 2 * SLOTS, width), BF16)] * 2
            + weight_space
            + [pltpu.SemaphoreType.DMA((count,)), pltpu.SemaphoreType.DMA((3, CHUNKS)), pltpu.SemaphoreType.DMA((count,))],
            input_output_aliases={4: 0} if main_out else {},
            compiler_params=params(60),
            cost_estimate=expert_cost(count * 2 * groups * SLOTS, width, hidden),
            name="main_expert",
        )(arrival, gate_proj, up_proj, down_proj, *main_out)

    main_out = main_expert(late_in, early_chips, late_chips, main_expert(early_in, 0, early_chips))
    main_back = lax.all_to_all(
        main_out.reshape(experts, SLOTS, width), ("node", "local"), split_axis=0, concat_axis=0, tiled=True
    )

    blocks = spill_back.reshape(groups, SLOTS, width)
    rolled = lax.dynamic_slice_in_dim(jnp.concatenate([blocks, blocks], axis=0), my_node, groups, axis=0)
    home = [rolled[0]]
    for hop in range(1, groups):
        home.append(lax.ppermute(rolled[hop], "node", [(i, (i + hop) % groups) for i in range(groups)]))
    spill_home = jnp.concatenate(home, axis=0)

    main_w, spill_w = pl.pallas_call(
        functools.partial(weight_kernel, groups, experts),
        in_specs=[whole(), whole()],
        out_specs=[whole(), whole()],
        out_shape=[
            jax.ShapeDtypeStruct((experts * SLOTS, tokens), BF16),
            jax.ShapeDtypeStruct((groups * SLOTS, tokens), BF16),
        ],
        compiler_params=params(16),
        name="combine_weights",
    )(id_rows, gate_rows)
    senders = (my_node - jnp.arange(groups, dtype=jnp.int32)) % groups
    spill_w = jnp.take(spill_w.reshape(groups, SLOTS, tokens), senders, axis=0).reshape(groups * SLOTS, tokens)

    return pl.pallas_call(
        combine_kernel,
        grid=(width // columns,),
        in_specs=[
            pl.BlockSpec((experts * SLOTS, tokens), lambda i: (0, 0)),
            pl.BlockSpec((groups * SLOTS, tokens), lambda i: (0, 0)),
            pl.BlockSpec((experts * SLOTS, columns), lambda i: (0, i)),
            pl.BlockSpec((groups * SLOTS, columns), lambda i: (0, i)),
        ],
        out_specs=pl.BlockSpec((tokens, columns), lambda i: (0, i)),
        out_shape=jax.ShapeDtypeStruct((tokens, width), BF16),
        compiler_params=params(60),
        name="combine",
    )(main_w, spill_w, main_back.reshape(experts * SLOTS, width), spill_home)


def solution(mesh):
    rows = P(("node", "local"), None)
    stacks = P(("node", "local"), None, None)
    return jax.shard_map(
        shards, mesh=mesh, in_specs=(rows, rows, rows, stacks, stacks, stacks), out_specs=rows, check_vma=False
    )
```

```python
import functools

import jax
import jax.numpy as jnp
from jax import lax
from jax.experimental import pallas as pl
from jax.experimental.pallas import tpu as pltpu
from jax.sharding import PartitionSpec as P

SLOTS = 8
EXTRA = 4
SHIFT = 3
BF16 = jnp.bfloat16
F32 = jnp.float32


def iota(shape, dim):
    return lax.broadcasted_iota(jnp.int32, shape, dim)


def indicator(mask):
    return jnp.where(mask, 1.0, 0.0).astype(F32)


def dot(left, right):
    return jnp.dot(left, right, preferred_element_type=F32)


def ranks_of(named):
    tokens = named.shape[1]
    earlier = indicator(iota((tokens, tokens), 0) < iota((tokens, tokens), 1))
    return dot(named.astype(BF16), earlier.astype(BF16))


def spread(values, flip):
    labels = values.shape[0]
    owner = (iota((labels * SLOTS, labels), 0) >> SHIFT) ^ flip
    picks = indicator(owner == iota((labels * SLOTS, labels), 1))
    return dot(picks.astype(BF16), values.astype(BF16))


def marks_of(ids_ref, labels):
    total = indicator(labels == ids_ref[0:1, :])
    for entry in range(1, ids_ref.shape[0]):
        total = total + indicator(labels == ids_ref[entry : entry + 1, :])
    return total


def slot_of(shape):
    return (iota(shape, 0) & (SLOTS - 1)).astype(F32)


def extra_of(shape):
    return (iota(shape, 0) & (EXTRA - 1)).astype(F32)


def first_half(shape):
    return (iota(shape, 0) & EXTRA) == 0


def send_kernel(ids_ref, acts_ref, out_ref, ranks):
    tokens, width = acts_ref.shape
    experts = ranks.shape[0]
    block = out_ref.shape[0]
    half = width // 2

    @pl.when(pl.program_id(0) == 0)
    def _():
        named = marks_of(ids_ref, iota((experts, tokens), 0))
        ranks[...] = jnp.where(named > 0.0, ranks_of(named), 99.0)

    mine = ranks[pl.ds(pl.multiple_of(pl.program_id(0) * block, block), block)]
    own = spread(mine, 0)
    other = spread(mine, 1)
    main = indicator(own == slot_of(own.shape)).astype(BF16)
    place = extra_of(own.shape)
    extra = jnp.maximum(indicator(own == place + SLOTS), indicator(other == place + (SLOTS + EXTRA)))
    low = jnp.where(first_half(own.shape), extra, 0.0).astype(BF16)
    high = jnp.where(first_half(own.shape), 0.0, extra).astype(BF16)
    rows = dot(main, acts_ref[...])
    out_ref[:, :, :width] = rows.reshape(block, SLOTS, width).astype(BF16)
    folded = dot(low, acts_ref[:, :half]) + dot(high, acts_ref[:, half:])
    out_ref[:, :, width:] = folded.reshape(block, SLOTS, half).astype(BF16)


def weight_kernel(ids_ref, gates_ref, main_ref, extra_ref):
    tokens = ids_ref.shape[1]
    experts = main_ref.shape[0] // SLOTS
    labels = iota((experts, tokens), 0)
    named = marks_of(ids_ref, labels)
    gates = jnp.zeros((experts, tokens), F32)
    for entry in range(ids_ref.shape[0]):
        value = gates_ref[entry : entry + 1, :].astype(F32)
        gates = gates + jnp.where(labels == ids_ref[entry : entry + 1, :], value, 0.0)
    ranks = jnp.where(named > 0.0, ranks_of(named), 99.0)
    own = spread(ranks, 0)
    own_gates = spread(gates, 0)
    main_ref[...] = jnp.where(own == slot_of(own.shape), own_gates, 0.0).astype(BF16)
    place = extra_of(own.shape)
    extra = jnp.where(own == place + SLOTS, own_gates, 0.0)
    extra += jnp.where(spread(ranks, 1) == place + (SLOTS + EXTRA), spread(gates, 1), 0.0)
    extra_ref[0] = jnp.where(first_half(own.shape), extra, 0.0).astype(BF16)
    extra_ref[1] = jnp.where(first_half(own.shape), 0.0, extra).astype(BF16)


CHUNKS = 4


def expert_loads(sources, weights, sems):
    loads = []
    for place, (source, weight) in enumerate(zip(sources, weights)):
        rows = weight.shape[0] // CHUNKS
        loads.append(
            [
                pltpu.make_async_copy(
                    source.at[0, pl.ds(part * rows, rows)], weight.at[pl.ds(part * rows, rows)], sems.at[place, part]
                )
                for part in range(CHUNKS)
            ]
        )
    return loads


def wait_all(copies):
    for copy in copies:
        copy.wait()


def expert_rows(blocks, weights, loads):
    gate_w, up_w, down_w = weights
    if loads:
        wait_all(loads[0])
    gates = [dot(rows(), gate_w[...]) for rows in blocks]
    if loads:
        wait_all(loads[1])
    ups = [dot(rows(), up_w[...]) for rows in blocks]
    hidden = [(g / (1.0 + jnp.exp(-g)) * u).astype(BF16) for g, u in zip(gates, ups)]
    if loads:
        wait_all(loads[2])
    return [dot(rows, down_w[...]).astype(BF16) for rows in hidden]


def unfold(folded):
    shape = (folded.shape[0] // 2, folded.shape[0])
    row = iota(shape, 0)
    start = (row >> 2) * SLOTS + (row & (EXTRA - 1))
    low = indicator(iota(shape, 1) == start).astype(BF16)
    high = indicator(iota(shape, 1) == start + EXTRA).astype(BF16)
    return jnp.concatenate([dot(low, folded).astype(BF16), dot(high, folded).astype(BF16)], axis=1)


def fold(rows):
    half = rows.shape[1] // 2
    shape = (rows.shape[0] * 2, rows.shape[0])
    source = (iota(shape, 0) >> SHIFT) * EXTRA + (iota(shape, 0) & (EXTRA - 1))
    match = iota(shape, 1) == source
    low = indicator(match & first_half(shape)).astype(BF16)
    high = indicator(match & jnp.logical_not(first_half(shape))).astype(BF16)
    return (dot(low, rows[:, :half]) + dot(high, rows[:, half:])).astype(BF16)


def expert_kernel(mode_ref, rows_hbm, *refs):
    sources = refs[:3], refs[3:6]
    out_hbm, held, done = refs[6:9]
    weights = refs[9:12], refs[12:15]
    row_sems, sems, out_sems = refs[15:]
    blocks, count, slots, full = held.shape
    width = weights[0][0].shape[0]
    half = width // 2
    mode = mode_ref[0]
    loads = [expert_loads(sources[side], weights[side], sems.at[side]) for side in range(2)]
    rows = [
        pltpu.make_async_copy(rows_hbm.at[pl.ds(block * count, count)], held.at[block], row_sems.at[block])
        for block in range(blocks)
    ]
    stores = [
        pltpu.make_async_copy(done.at[block], out_hbm.at[pl.ds(block * count, count)], out_sems.at[block])
        for block in range(blocks)
    ]
    for copy in rows[:2] + loads[0][0] + loads[0][1] + rows[2:] + loads[0][2]:
        copy.start()

    @pl.when(mode == 2)
    def _():
        for copy in loads[1][0] + loads[1][1] + loads[1][2]:
            copy.start()

    for pair in range(0, blocks, 2):
        wait_all(rows[pair : pair + 2])
        both = [lambda b=b: held[b, :, :, :width].reshape(count * slots, width) for b in (pair, pair + 1)]
        results = expert_rows(both, weights[0], loads[0] if pair == 0 else None)
        for block, result in zip((pair, pair + 1), results):
            done[block, :, :, :width] = result.reshape(count, slots, width)

    def extras(side):
        if side:
            wait_all(loads[1][0] + loads[1][1] + loads[1][2])
        parts = [unfold(held[block, :, :, width:].reshape(count * slots, half)) for block in range(blocks)]
        both = [lambda a=a: jnp.concatenate(parts[a : a + 2], axis=0) for a in range(0, blocks, 2)]
        results = expert_rows(both, weights[side], None)
        for block in range(blocks):
            start = (block % 2) * count * EXTRA
            result = results[block // 2][start : start + count * EXTRA]
            done[block, :, :, width:] = fold(result).reshape(count, slots, half)

    for side in range(2):

        @pl.when(mode == side + 1)
        def _():
            extras(side)

    @pl.when(mode == 0)
    def _():
        done[:, :, :, width:] = jnp.zeros((blocks, count, slots, half), BF16)

    for store in stores:
        store.start()
    wait_all(stores)


def combine_kernel(main_w_ref, extra_w_ref, main_ref, extra_ref, out_ref):
    over_rows = (((0,), (0,)), ((), ()))
    total = lax.dot_general(main_w_ref[...], main_ref[...], over_rows, preferred_element_type=F32)
    total += lax.dot_general(extra_w_ref[0], extra_ref[...], over_rows, preferred_element_type=F32)
    out_ref[...] = total.astype(BF16)


def params(megabytes):
    return pltpu.CompilerParams(vmem_limit_bytes=megabytes * 1024 * 1024)


def whole():
    return pl.BlockSpec(memory_space=pltpu.VMEM)


def hbm():
    return pl.BlockSpec(memory_space=pltpu.HBM)


def shards(activations, expert_ids, route_gates, gate_proj, up_proj, down_proj):
    tokens, width = activations.shape
    top = expert_ids.shape[1]
    hidden = gate_proj.shape[2]
    groups = lax.axis_size("node")
    per_group = lax.axis_size("local")
    experts = groups * per_group
    half = width // 2
    full = width + half
    my_expert = (lax.axis_index("node") * per_group + lax.axis_index("local")).astype(jnp.int32)
    id_rows = expert_ids.T
    gate_rows = route_gates.T

    block = experts // 4
    sent = pl.pallas_call(
        send_kernel,
        grid=(experts // block,),
        in_specs=[
            pl.BlockSpec((top, tokens), lambda i: (0, 0)),
            pl.BlockSpec((tokens, width), lambda i: (0, 0)),
        ],
        out_specs=pl.BlockSpec((block, SLOTS, full), lambda i: (i, 0, 0)),
        out_shape=jax.ShapeDtypeStruct((experts, SLOTS, full), BF16),
        scratch_shapes=[pltpu.VMEM((experts, tokens), F32)],
        compiler_params=params(60),
        name="send_rows",
    )(id_rows, activations)

    def exchange(rows):
        return lax.all_to_all(rows, ("node", "local"), split_axis=0, concat_axis=0, tiled=True)

    arrived = exchange(sent)
    cores = [(i, i ^ 1) for i in range(per_group)]
    other = [lax.ppermute(weight, "local", cores) for weight in (gate_proj, up_proj, down_proj)]

    mine = jnp.sum((expert_ids == my_expert).astype(jnp.int32)) > SLOTS
    theirs = jnp.sum((expert_ids == (my_expert ^ 1)).astype(jnp.int32)) > SLOTS
    mode = jnp.where(mine, 1, jnp.where(theirs, 2, 0)).astype(jnp.int32).reshape(1)
    weight_space = [
        pltpu.VMEM((width, hidden), BF16),
        pltpu.VMEM((width, hidden), BF16),
        pltpu.VMEM((hidden, width), BF16),
    ]
    count = experts * SLOTS
    results = pl.pallas_call(
        expert_kernel,
        in_specs=[pl.BlockSpec(memory_space=pltpu.SMEM)] + [hbm()] * 7,
        out_specs=hbm(),
        out_shape=jax.ShapeDtypeStruct((experts, SLOTS, full), BF16),
        scratch_shapes=[pltpu.VMEM((4, experts // 4, SLOTS, full), BF16)] * 2
        + weight_space * 2
        + [pltpu.SemaphoreType.DMA((4,)), pltpu.SemaphoreType.DMA((2, 3, CHUNKS)), pltpu.SemaphoreType.DMA((4,))],
        compiler_params=params(60),
        cost_estimate=pl.CostEstimate(
            flops=9 * count * width * hidden,
            bytes_accessed=6 * count * width + 12 * width * hidden,
            transcendentals=2 * count * hidden,
        ),
        name="expert",
    )(mode, arrived, gate_proj, up_proj, down_proj, *other)

    main_w, extra_w = pl.pallas_call(
        weight_kernel,
        in_specs=[whole(), whole()],
        out_specs=[whole(), whole()],
        out_shape=[
            jax.ShapeDtypeStruct((count, tokens), BF16),
            jax.ShapeDtypeStruct((2, count, tokens), BF16),
        ],
        compiler_params=params(24),
        name="combine_weights",
    )(id_rows, gate_rows)

    returned = exchange(results).reshape(count, full)
    return pl.pallas_call(
        combine_kernel,
        grid=(2,),
        in_specs=[
            pl.BlockSpec((count, tokens), lambda i: (0, 0)),
            pl.BlockSpec((1, count, tokens), lambda i: (i, 0, 0)),
            pl.BlockSpec((count, half), lambda i: (0, i)),
            pl.BlockSpec((count, half), lambda i: (0, 2)),
        ],
        out_specs=pl.BlockSpec((tokens, half), lambda i: (0, i)),
        out_shape=jax.ShapeDtypeStruct((tokens, width), BF16),
        compiler_params=params(60),
        name="combine",
    )(main_w, extra_w, returned, returned)


def solution(mesh):
    rows = P(("node", "local"), None)
    stacks = P(("node", "local"), None, None)
    return jax.shard_map(
        shards, mesh=mesh, in_specs=(rows, rows, rows, stacks, stacks, stacks), out_specs=rows, check_vma=False
    )
```

```python
import functools

import jax
import jax.numpy as jnp
from jax import lax
from jax.experimental import pallas as pl
from jax.experimental.pallas import tpu as pltpu
from jax.sharding import PartitionSpec as P

SLOTS = 8
EXTRA = 4
SHIFT = 3
BF16 = jnp.bfloat16
F32 = jnp.float32


def iota(shape, dim):
    return lax.broadcasted_iota(jnp.int32, shape, dim)


def indicator(mask):
    return jnp.where(mask, 1.0, 0.0).astype(F32)


def dot(left, right):
    return jnp.dot(left, right, preferred_element_type=F32)


def ranks_of(named):
    tokens = named.shape[1]
    earlier = indicator(iota((tokens, tokens), 0) < iota((tokens, tokens), 1))
    return dot(named.astype(BF16), earlier.astype(BF16))


def spread(values, flip):
    labels = values.shape[0]
    owner = (iota((labels * SLOTS, labels), 0) >> SHIFT) ^ flip
    picks = indicator(owner == iota((labels * SLOTS, labels), 1))
    return dot(picks.astype(BF16), values.astype(BF16))


def marks_of(ids_ref, labels):
    total = indicator(labels == ids_ref[0:1, :])
    for entry in range(1, ids_ref.shape[0]):
        total = total + indicator(labels == ids_ref[entry : entry + 1, :])
    return total


def slot_of(shape):
    return (iota(shape, 0) & (SLOTS - 1)).astype(F32)


def extra_of(shape):
    return (iota(shape, 0) & (EXTRA - 1)).astype(F32)


def first_half(shape):
    return (iota(shape, 0) & EXTRA) == 0


def send_kernel(ids_ref, acts_ref, out_ref, ranks):
    tokens, width = acts_ref.shape
    experts = ranks.shape[0]
    block = out_ref.shape[0]
    half = width // 2

    @pl.when(pl.program_id(0) == 0)
    def _():
        named = marks_of(ids_ref, iota((experts, tokens), 0))
        ranks[...] = jnp.where(named > 0.0, ranks_of(named), 99.0)

    mine = ranks[pl.ds(pl.multiple_of(pl.program_id(0) * block, block), block)]
    own = spread(mine, 0)
    other = spread(mine, 1)
    main = indicator(own == slot_of(own.shape)).astype(BF16)
    place = extra_of(own.shape)
    extra = jnp.maximum(indicator(own == place + SLOTS), indicator(other == place + (SLOTS + EXTRA)))
    low = jnp.where(first_half(own.shape), extra, 0.0).astype(BF16)
    high = jnp.where(first_half(own.shape), 0.0, extra).astype(BF16)
    rows = dot(main, acts_ref[...])
    out_ref[:, :, :width] = rows.reshape(block, SLOTS, width).astype(BF16)
    folded = dot(low, acts_ref[:, :half]) + dot(high, acts_ref[:, half:])
    out_ref[:, :, width:] = folded.reshape(block, SLOTS, half).astype(BF16)


def weight_kernel(ids_ref, gates_ref, main_ref, extra_ref):
    tokens = ids_ref.shape[1]
    experts = main_ref.shape[0] // SLOTS
    labels = iota((experts, tokens), 0)
    named = marks_of(ids_ref, labels)
    gates = jnp.zeros((experts, tokens), F32)
    for entry in range(ids_ref.shape[0]):
        value = gates_ref[entry : entry + 1, :].astype(F32)
        gates = gates + jnp.where(labels == ids_ref[entry : entry + 1, :], value, 0.0)
    ranks = jnp.where(named > 0.0, ranks_of(named), 99.0)
    own = spread(ranks, 0)
    own_gates = spread(gates, 0)
    main_ref[...] = jnp.where(own == slot_of(own.shape), own_gates, 0.0).astype(BF16)
    place = extra_of(own.shape)
    extra = jnp.where(own == place + SLOTS, own_gates, 0.0)
    extra += jnp.where(spread(ranks, 1) == place + (SLOTS + EXTRA), spread(gates, 1), 0.0)
    extra_ref[0] = jnp.where(first_half(own.shape), extra, 0.0).astype(BF16)
    extra_ref[1] = jnp.where(first_half(own.shape), 0.0, extra).astype(BF16)


def wait_all(copies):
    for copy in copies:
        copy.wait()


CHUNKS = 4


def expert_loads(sources, weights, sems):
    loads = []
    for place, (source, weight) in enumerate(zip(sources, weights)):
        rows = weight.shape[0] // CHUNKS
        for part in range(CHUNKS):
            there = pl.ds(part * rows, rows)
            loads.append(pltpu.make_async_copy(source.at[0, there], weight.at[there], sems.at[place, part]))
    return loads


def expert_rows(blocks, weights, loads=None):
    gate_w, up_w, down_w = weights
    if loads:
        wait_all(loads[:CHUNKS])
    gates = [dot(rows, gate_w[...]) for rows in blocks]
    if loads:
        wait_all(loads[CHUNKS : 2 * CHUNKS])
    ups = [dot(rows, up_w[...]) for rows in blocks]
    hidden = [(g / (1.0 + jnp.exp(-g)) * u).astype(BF16) for g, u in zip(gates, ups)]
    if loads:
        wait_all(loads[2 * CHUNKS :])
    return [dot(rows, down_w[...]).astype(BF16) for rows in hidden]


def unfold(folded):
    shape = (folded.shape[0] // 2, folded.shape[0])
    row = iota(shape, 0)
    start = (row >> 2) * SLOTS + (row & (EXTRA - 1))
    low = indicator(iota(shape, 1) == start).astype(BF16)
    high = indicator(iota(shape, 1) == start + EXTRA).astype(BF16)
    return jnp.concatenate([dot(low, folded).astype(BF16), dot(high, folded).astype(BF16)], axis=1)


def fold(rows):
    half = rows.shape[1] // 2
    shape = (rows.shape[0] * 2, rows.shape[0])
    source = (iota(shape, 0) >> SHIFT) * EXTRA + (iota(shape, 0) & (EXTRA - 1))
    match = iota(shape, 1) == source
    low = indicator(match & first_half(shape)).astype(BF16)
    high = indicator(match & jnp.logical_not(first_half(shape))).astype(BF16)
    return (dot(low, rows[:, :half]) + dot(high, rows[:, half:])).astype(BF16)


def expert_kernel(mode_ref, rows_hbm, *refs):
    out_hbm, held, held_extra, done, done_extra = refs[6:11]
    weights = refs[11:14], refs[14:17]
    row_sems, out_sems, sems = refs[17:]
    blocks, count, slots, width = held.shape
    half = width // 2
    mode = mode_ref[0]

    def moves(block):
        there = pl.ds(block * count, count)
        main, extra = pl.ds(0, width), pl.ds(width, half)
        return (
            pltpu.make_async_copy(rows_hbm.at[there, :, main], held.at[block], row_sems.at[0, block]),
            pltpu.make_async_copy(rows_hbm.at[there, :, extra], held_extra.at[block], row_sems.at[1, block]),
            pltpu.make_async_copy(done.at[block], out_hbm.at[there, :, main], out_sems.at[0, block]),
            pltpu.make_async_copy(done_extra.at[block], out_hbm.at[there, :, extra], out_sems.at[1, block]),
        )

    rows, extra_rows, stores, extra_stores = zip(*[moves(block) for block in range(blocks)])
    loads = [expert_loads(refs[3 * side : 3 * side + 3], weights[side], sems.at[side]) for side in range(2)]
    for copy in [*rows[:2], *loads[0][: 2 * CHUNKS], *rows[2:], *loads[0][2 * CHUNKS :], *extra_rows]:
        copy.start()

    @pl.when(mode == 0)
    def _():
        done_extra[...] = jnp.zeros(done_extra.shape, BF16)
        for store in extra_stores:
            store.start()

    for pair in range(0, blocks, 2):
        wait_all(rows[pair : pair + 2])
        both = [held[block].reshape(count * slots, width) for block in (pair, pair + 1)]
        results = expert_rows(both, weights[0], loads[0] if pair == 0 else None)
        for block, result in zip((pair, pair + 1), results):
            done[block] = result.reshape(count, slots, width)
            stores[block].start()
        if pair == 0:

            @pl.when(mode == 2)
            def _():
                for copy in loads[1]:
                    copy.start()

    wait_all(extra_rows)

    def extras(side):
        if side:
            wait_all(loads[1])
        parts = [unfold(held_extra[block].reshape(count * slots, half)) for block in range(blocks)]
        both = [jnp.concatenate(parts[a : a + 2], axis=0) for a in range(0, blocks, 2)]
        results = expert_rows(both, weights[side])
        for block in range(blocks):
            start = (block % 2) * count * EXTRA
            result = results[block // 2][start : start + count * EXTRA]
            done_extra[block] = fold(result).reshape(count, slots, half)
            extra_stores[block].start()

    for side in range(2):

        @pl.when(mode == side + 1)
        def _():
            extras(side)

    wait_all(stores + extra_stores)


def combine_kernel(main_w_ref, extra_w_ref, main_ref, extra_ref, out_ref):
    over_rows = (((0,), (0,)), ((), ()))
    total = lax.dot_general(main_w_ref[...], main_ref[...], over_rows, preferred_element_type=F32)
    total += lax.dot_general(extra_w_ref[0], extra_ref[...], over_rows, preferred_element_type=F32)
    out_ref[...] = total.astype(BF16)


def params(megabytes):
    return pltpu.CompilerParams(vmem_limit_bytes=megabytes * 1024 * 1024)


def whole():
    return pl.BlockSpec(memory_space=pltpu.VMEM)


def hbm():
    return pl.BlockSpec(memory_space=pltpu.HBM)


def shards(activations, expert_ids, route_gates, gate_proj, up_proj, down_proj):
    tokens, width = activations.shape
    top = expert_ids.shape[1]
    hidden = gate_proj.shape[2]
    groups = lax.axis_size("node")
    per_group = lax.axis_size("local")
    experts = groups * per_group
    half = width // 2
    full = width + half
    my_expert = (lax.axis_index("node") * per_group + lax.axis_index("local")).astype(jnp.int32)
    id_rows = expert_ids.T
    gate_rows = route_gates.T

    block = experts // 4
    sent = pl.pallas_call(
        send_kernel,
        grid=(experts // block,),
        in_specs=[
            pl.BlockSpec((top, tokens), lambda i: (0, 0)),
            pl.BlockSpec((tokens, width), lambda i: (0, 0)),
        ],
        out_specs=pl.BlockSpec((block, SLOTS, full), lambda i: (i, 0, 0)),
        out_shape=jax.ShapeDtypeStruct((experts, SLOTS, full), BF16),
        scratch_shapes=[pltpu.VMEM((experts, tokens), F32)],
        compiler_params=params(60),
        name="send_rows",
    )(id_rows, activations)

    def exchange(rows):
        return lax.all_to_all(rows, ("node", "local"), split_axis=0, concat_axis=0, tiled=True)

    arrived = exchange(sent)
    cores = [(i, i ^ 1) for i in range(per_group)]
    other = [lax.ppermute(weight, "local", cores) for weight in (gate_proj, up_proj, down_proj)]

    mine = jnp.sum((expert_ids == my_expert).astype(jnp.int32)) > SLOTS
    theirs = jnp.sum((expert_ids == (my_expert ^ 1)).astype(jnp.int32)) > SLOTS
    mode = jnp.where(mine, 1, jnp.where(theirs, 2, 0)).astype(jnp.int32).reshape(1)
    count = experts * SLOTS
    weight_shapes = [(width, hidden), (width, hidden), (hidden, width)]
    results = pl.pallas_call(
        expert_kernel,
        in_specs=[pl.BlockSpec(memory_space=pltpu.SMEM), hbm()] + [hbm()] * 6,
        out_specs=hbm(),
        out_shape=jax.ShapeDtypeStruct((experts, SLOTS, full), BF16),
        scratch_shapes=[
            pltpu.VMEM((4, experts // 4, SLOTS, width), BF16),
            pltpu.VMEM((4, experts // 4, SLOTS, half), BF16),
        ]
        * 2
        + [pltpu.VMEM(shape, BF16) for shape in weight_shapes] * 2
        + [pltpu.SemaphoreType.DMA((2, 4)), pltpu.SemaphoreType.DMA((2, 4)), pltpu.SemaphoreType.DMA((2, 3, CHUNKS))],
        compiler_params=params(60),
        cost_estimate=pl.CostEstimate(
            flops=9 * count * width * hidden,
            bytes_accessed=6 * count * width + 12 * width * hidden,
            transcendentals=2 * count * hidden,
        ),
        name="expert",
    )(mode, arrived, gate_proj, up_proj, down_proj, *other)

    main_w, extra_w = pl.pallas_call(
        weight_kernel,
        in_specs=[whole(), whole()],
        out_specs=[whole(), whole()],
        out_shape=[
            jax.ShapeDtypeStruct((count, tokens), BF16),
            jax.ShapeDtypeStruct((2, count, tokens), BF16),
        ],
        compiler_params=params(24),
        name="combine_weights",
    )(id_rows, gate_rows)

    returned = exchange(results).reshape(count, full)
    return pl.pallas_call(
        combine_kernel,
        grid=(2, 2),
        in_specs=[
            pl.BlockSpec((count, tokens), lambda j, side: (0, 0)),
            pl.BlockSpec((1, count, tokens), lambda j, side: (side, 0, 0)),
            pl.BlockSpec((count, half // 2), lambda j, side: (0, 2 * side + j)),
            pl.BlockSpec((count, half // 2), lambda j, side: (0, 4 + j)),
        ],
        out_specs=pl.BlockSpec((tokens, half // 2), lambda j, side: (0, 2 * side + j)),
        out_shape=jax.ShapeDtypeStruct((tokens, width), BF16),
        compiler_params=params(60),
        name="combine",
    )(main_w, extra_w, returned, returned)


def solution(mesh):
    rows = P(("node", "local"), None)
    stacks = P(("node", "local"), None, None)
    return jax.shard_map(
        shards, mesh=mesh, in_specs=(rows, rows, rows, stacks, stacks, stacks), out_specs=rows, check_vma=False
    )
```

```python
import functools

import jax
import jax.numpy as jnp
from jax import lax
from jax.experimental import pallas as pl
from jax.experimental.pallas import tpu as pltpu
from jax.sharding import PartitionSpec as P

SLOTS = 8
EXTRA = 4
SHIFT = 3
BF16 = jnp.bfloat16
F32 = jnp.float32


def iota(shape, dim):
    return lax.broadcasted_iota(jnp.int32, shape, dim)


def indicator(mask):
    return jnp.where(mask, 1.0, 0.0).astype(F32)


def dot(left, right):
    return jnp.dot(left, right, preferred_element_type=F32)


def ranks_of(named):
    tokens = named.shape[1]
    earlier = indicator(iota((tokens, tokens), 0) < iota((tokens, tokens), 1))
    return dot(named.astype(BF16), earlier.astype(BF16))


def spread(values, flip):
    labels = values.shape[0]
    owner = (iota((labels * SLOTS, labels), 0) >> SHIFT) ^ flip
    picks = indicator(owner == iota((labels * SLOTS, labels), 1))
    return dot(picks.astype(BF16), values.astype(BF16))


def marks_of(ids_ref, labels):
    total = indicator(labels == ids_ref[0:1, :])
    for entry in range(1, ids_ref.shape[0]):
        total = total + indicator(labels == ids_ref[entry : entry + 1, :])
    return total


def slot_of(shape):
    return (iota(shape, 0) & (SLOTS - 1)).astype(F32)


def extra_of(shape):
    return (iota(shape, 0) & (EXTRA - 1)).astype(F32)


def first_half(shape):
    return (iota(shape, 0) & EXTRA) == 0


def send_kernel(ids_ref, acts_ref, out_ref, main_picks, extra_picks, stacked):
    tokens, width = acts_ref.shape
    count = main_picks.shape[0]
    block = out_ref.shape[0]
    half = width // 2

    @pl.when(pl.program_id(0) == 0)
    def _():
        named = marks_of(ids_ref, iota((count // SLOTS, tokens), 0))
        ranks = jnp.where(named > 0.0, ranks_of(named), 99.0)
        own = spread(ranks, 0)
        other = spread(ranks, 1)
        main_picks[...] = indicator(own == slot_of(own.shape)).astype(BF16)
        place = extra_of(own.shape)
        extra = jnp.maximum(indicator(own == place + SLOTS), indicator(other == place + (SLOTS + EXTRA)))
        extra_picks[:, :tokens] = jnp.where(first_half(own.shape), extra, 0.0).astype(BF16)
        extra_picks[:, tokens:] = jnp.where(first_half(own.shape), 0.0, extra).astype(BF16)
        stacked[:tokens] = acts_ref[:, :half]
        stacked[tokens:] = acts_ref[:, half:]

    here = pl.ds(pl.multiple_of(pl.program_id(0) * block * SLOTS, block * SLOTS), block * SLOTS)
    rows = dot(main_picks[here], acts_ref[...])
    out_ref[:, :, :width] = rows.reshape(block, SLOTS, width).astype(BF16)
    folded = dot(extra_picks[here], stacked[...])
    out_ref[:, :, width:] = folded.reshape(block, SLOTS, half).astype(BF16)


def weight_kernel(ids_ref, gates_ref, main_ref, extra_ref):
    tokens = ids_ref.shape[1]
    experts = main_ref.shape[1] // SLOTS
    labels = iota((experts, tokens), 0)
    named = marks_of(ids_ref, labels)
    gates = jnp.zeros((experts, tokens), F32)
    for entry in range(ids_ref.shape[0]):
        value = gates_ref[entry : entry + 1, :].astype(F32)
        gates = gates + jnp.where(labels == ids_ref[entry : entry + 1, :], value, 0.0)
    ranks = jnp.where(named > 0.0, ranks_of(named), 99.0)
    own = spread(ranks, 0)
    own_gates = spread(gates, 0)
    main_ref[...] = jnp.where(own == slot_of(own.shape), own_gates, 0.0).T.astype(BF16)
    place = extra_of(own.shape)
    extra = jnp.where(own == place + SLOTS, own_gates, 0.0)
    extra += jnp.where(spread(ranks, 1) == place + (SLOTS + EXTRA), spread(gates, 1), 0.0)
    extra_ref[0] = jnp.where(first_half(own.shape), extra, 0.0).T.astype(BF16)
    extra_ref[1] = jnp.where(first_half(own.shape), 0.0, extra).T.astype(BF16)


def wait_all(copies):
    for copy in copies:
        copy.wait()


CHUNKS = 4


def expert_loads(sources, weights, sems):
    loads = []
    for place, (source, weight) in enumerate(zip(sources, weights)):
        rows = weight.shape[0] // CHUNKS
        for part in range(CHUNKS):
            there = pl.ds(part * rows, rows)
            loads.append(pltpu.make_async_copy(source.at[0, there], weight.at[there], sems.at[place, part]))
    return loads


def expert_rows(blocks, weights, loads=None):
    gate_w, up_w, down_w = weights
    if loads:
        wait_all(loads[:CHUNKS])
    gates = [dot(rows, gate_w[...]) for rows in blocks]
    if loads:
        wait_all(loads[CHUNKS : 2 * CHUNKS])
    ups = [dot(rows, up_w[...]) for rows in blocks]
    hidden = [(g / (1.0 + jnp.exp(-g)) * u).astype(BF16) for g, u in zip(gates, ups)]
    if loads:
        wait_all(loads[2 * CHUNKS :])
    return [dot(rows, down_w[...]).astype(BF16) for rows in hidden]


def unfold(folded):
    shape = (folded.shape[0] // 2, folded.shape[0])
    row = iota(shape, 0)
    start = (row >> 2) * SLOTS + (row & (EXTRA - 1))
    low = indicator(iota(shape, 1) == start).astype(BF16)
    high = indicator(iota(shape, 1) == start + EXTRA).astype(BF16)
    return jnp.concatenate([dot(low, folded).astype(BF16), dot(high, folded).astype(BF16)], axis=1)


def fold(rows):
    half = rows.shape[1] // 2
    shape = (rows.shape[0] * 2, rows.shape[0])
    source = (iota(shape, 0) >> SHIFT) * EXTRA + (iota(shape, 0) & (EXTRA - 1))
    match = iota(shape, 1) == source
    low = indicator(match & first_half(shape)).astype(BF16)
    high = indicator(match & jnp.logical_not(first_half(shape))).astype(BF16)
    return (dot(low, rows[:, :half]) + dot(high, rows[:, half:])).astype(BF16)


def expert_kernel(mode_ref, rows_hbm, *refs):
    out_hbm, held, held_extra, done, done_extra = refs[6:11]
    weights = refs[11:14], refs[14:17]
    row_sems, out_sems, sems = refs[17:]
    blocks, count, slots, width = held.shape
    half = width // 2
    mode = mode_ref[0]

    def moves(block):
        there = pl.ds(block * count, count)
        main, extra = pl.ds(0, width), pl.ds(width, half)
        return (
            pltpu.make_async_copy(rows_hbm.at[there, :, main], held.at[block], row_sems.at[0, block]),
            pltpu.make_async_copy(rows_hbm.at[there, :, extra], held_extra.at[block], row_sems.at[1, block]),
            pltpu.make_async_copy(done.at[block], out_hbm.at[there, :, main], out_sems.at[0, block]),
            pltpu.make_async_copy(done_extra.at[block], out_hbm.at[there, :, extra], out_sems.at[1, block]),
        )

    rows, extra_rows, stores, extra_stores = zip(*[moves(block) for block in range(blocks)])
    loads = [expert_loads(refs[3 * side : 3 * side + 3], weights[side], sems.at[side]) for side in range(2)]
    for copy in [*rows[:2], *loads[0][: 2 * CHUNKS], *rows[2:], *loads[0][2 * CHUNKS :], *extra_rows]:
        copy.start()

    @pl.when(mode == 0)
    def _():
        done_extra[...] = jnp.zeros(done_extra.shape, BF16)
        for store in extra_stores:
            store.start()

    for pair in range(0, blocks, 2):
        wait_all(rows[pair : pair + 2])
        both = [held[block].reshape(count * slots, width) for block in (pair, pair + 1)]
        results = expert_rows(both, weights[0], loads[0] if pair == 0 else None)
        for block, result in zip((pair, pair + 1), results):
            done[block] = result.reshape(count, slots, width)
            stores[block].start()
        if pair == 0:

            @pl.when(mode == 2)
            def _():
                for copy in loads[1]:
                    copy.start()

    wait_all(extra_rows)

    def extras(side):
        if side:
            wait_all(loads[1])
        parts = [unfold(held_extra[block].reshape(count * slots, half)) for block in range(blocks)]
        both = [jnp.concatenate(parts[a : a + 2], axis=0) for a in range(0, blocks, 2)]
        results = expert_rows(both, weights[side])
        for block in range(blocks):
            start = (block % 2) * count * EXTRA
            result = results[block // 2][start : start + count * EXTRA]
            done_extra[block] = fold(result).reshape(count, slots, half)
            extra_stores[block].start()

    for side in range(2):

        @pl.when(mode == side + 1)
        def _():
            extras(side)

    wait_all(stores + extra_stores)


def combine_kernel(main_w_ref, extra_w_ref, main_ref, extra_ref, out_ref):
    total = dot(main_w_ref[...], main_ref[...]) + dot(extra_w_ref[0], extra_ref[...])
    out_ref[...] = total.astype(BF16)


def params(megabytes):
    return pltpu.CompilerParams(vmem_limit_bytes=megabytes * 1024 * 1024)


def whole():
    return pl.BlockSpec(memory_space=pltpu.VMEM)


def hbm():
    return pl.BlockSpec(memory_space=pltpu.HBM)


def shards(activations, expert_ids, route_gates, gate_proj, up_proj, down_proj):
    tokens, width = activations.shape
    top = expert_ids.shape[1]
    hidden = gate_proj.shape[2]
    groups = lax.axis_size("node")
    per_group = lax.axis_size("local")
    experts = groups * per_group
    half = width // 2
    full = width + half
    my_expert = (lax.axis_index("node") * per_group + lax.axis_index("local")).astype(jnp.int32)
    id_rows = expert_ids.T
    gate_rows = route_gates.T

    block = experts // 4
    sent = pl.pallas_call(
        send_kernel,
        grid=(experts // block,),
        in_specs=[
            pl.BlockSpec((top, tokens), lambda i: (0, 0)),
            pl.BlockSpec((tokens, width), lambda i: (0, 0)),
        ],
        out_specs=pl.BlockSpec((block, SLOTS, full), lambda i: (i, 0, 0)),
        out_shape=jax.ShapeDtypeStruct((experts, SLOTS, full), BF16),
        scratch_shapes=[
            pltpu.VMEM((experts * SLOTS, tokens), BF16),
            pltpu.VMEM((experts * SLOTS, 2 * tokens), BF16),
            pltpu.VMEM((2 * tokens, half), BF16),
        ],
        compiler_params=params(60),
        name="send_rows",
    )(id_rows, activations)

    def exchange(rows):
        return lax.all_to_all(rows, ("node", "local"), split_axis=0, concat_axis=0, tiled=True)

    arrived = exchange(sent)
    cores = [(i, i ^ 1) for i in range(per_group)]
    other = [lax.ppermute(weight, "local", cores) for weight in (gate_proj, up_proj, down_proj)]

    mine = jnp.sum((expert_ids == my_expert).astype(jnp.int32)) > SLOTS
    theirs = jnp.sum((expert_ids == (my_expert ^ 1)).astype(jnp.int32)) > SLOTS
    mode = jnp.where(mine, 1, jnp.where(theirs, 2, 0)).astype(jnp.int32).reshape(1)
    count = experts * SLOTS
    weight_shapes = [(width, hidden), (width, hidden), (hidden, width)]
    results = pl.pallas_call(
        expert_kernel,
        in_specs=[pl.BlockSpec(memory_space=pltpu.SMEM), hbm()] + [hbm()] * 6,
        out_specs=hbm(),
        out_shape=jax.ShapeDtypeStruct((experts, SLOTS, full), BF16),
        scratch_shapes=[
            pltpu.VMEM((4, experts // 4, SLOTS, width), BF16),
            pltpu.VMEM((4, experts // 4, SLOTS, half), BF16),
        ]
        * 2
        + [pltpu.VMEM(shape, BF16) for shape in weight_shapes] * 2
        + [pltpu.SemaphoreType.DMA((2, 4)), pltpu.SemaphoreType.DMA((2, 4)), pltpu.SemaphoreType.DMA((2, 3, CHUNKS))],
        compiler_params=params(60),
        cost_estimate=pl.CostEstimate(
            flops=9 * count * width * hidden,
            bytes_accessed=6 * count * width + 12 * width * hidden,
            transcendentals=2 * count * hidden,
        ),
        name="expert",
    )(mode, arrived, gate_proj, up_proj, down_proj, *other)

    main_w, extra_w = pl.pallas_call(
        weight_kernel,
        in_specs=[whole(), whole()],
        out_specs=[whole(), whole()],
        out_shape=[
            jax.ShapeDtypeStruct((tokens, count), BF16),
            jax.ShapeDtypeStruct((2, tokens, count), BF16),
        ],
        compiler_params=params(24),
        name="combine_weights",
    )(id_rows, gate_rows)

    returned = exchange(results).reshape(count, full)
    return pl.pallas_call(
        combine_kernel,
        grid=(2, 2),
        in_specs=[
            pl.BlockSpec((tokens, count), lambda j, side: (0, 0)),
            pl.BlockSpec((1, tokens, count), lambda j, side: (side, 0, 0)),
            pl.BlockSpec((count, half // 2), lambda j, side: (0, 2 * side + j)),
            pl.BlockSpec((count, half // 2), lambda j, side: (0, 4 + j)),
        ],
        out_specs=pl.BlockSpec((tokens, half // 2), lambda j, side: (0, 2 * side + j)),
        out_shape=jax.ShapeDtypeStruct((tokens, width), BF16),
        compiler_params=params(60),
        name="combine",
    )(main_w, extra_w, returned, returned)


def solution(mesh):
    rows = P(("node", "local"), None)
    stacks = P(("node", "local"), None, None)
    return jax.shard_map(
        shards, mesh=mesh, in_specs=(rows, rows, rows, stacks, stacks, stacks), out_specs=rows, check_vma=False
    )
```

```python
import functools

import jax
import jax.numpy as jnp
from jax import lax
from jax.experimental import pallas as pl
from jax.experimental.pallas import tpu as pltpu
from jax.sharding import PartitionSpec as P

SLOTS = 8
EXTRA = 4
SHIFT = 3
BF16 = jnp.bfloat16
F32 = jnp.float32


def iota(shape, dim):
    return lax.broadcasted_iota(jnp.int32, shape, dim)


def indicator(mask):
    return jnp.where(mask, 1.0, 0.0).astype(F32)


def dot(left, right):
    return jnp.dot(left, right, preferred_element_type=F32)


def ranks_of(named):
    tokens = named.shape[1]
    earlier = indicator(iota((tokens, tokens), 0) < iota((tokens, tokens), 1))
    return dot(named.astype(BF16), earlier.astype(BF16))


def spread(values, flip):
    labels = values.shape[0]
    owner = (iota((labels * SLOTS, labels), 0) >> SHIFT) ^ flip
    picks = indicator(owner == iota((labels * SLOTS, labels), 1))
    return dot(picks.astype(BF16), values.astype(BF16))


def marks_of(ids_ref, labels):
    total = indicator(labels == ids_ref[0:1, :])
    for entry in range(1, ids_ref.shape[0]):
        total = total + indicator(labels == ids_ref[entry : entry + 1, :])
    return total


def slot_of(shape):
    return (iota(shape, 0) & (SLOTS - 1)).astype(F32)


def extra_of(shape):
    return (iota(shape, 0) & (EXTRA - 1)).astype(F32)


def first_half(shape):
    return (iota(shape, 0) & EXTRA) == 0


def wait_all(copies):
    for copy in copies:
        copy.wait()


def send_kernel(ids_hbm, acts_hbm, out_hbm, ids_ref, acts_ref, held, in_sems, out_sems):
    tokens, width = acts_ref.shape
    experts = held.shape[0]
    half = width // 2
    runs = out_sems.shape[0]
    run = experts // runs
    ids_copy = pltpu.make_async_copy(ids_hbm, ids_ref, in_sems.at[0])
    acts_copy = pltpu.make_async_copy(acts_hbm, acts_ref, in_sems.at[1])
    ids_copy.start()
    acts_copy.start()
    ids_copy.wait()
    named = marks_of(ids_ref, iota((experts, tokens), 0))
    ranks = jnp.where(named > 0.0, ranks_of(named), 99.0)
    own = spread(ranks, 0)
    other = spread(ranks, 1)
    main = indicator(own == slot_of(own.shape)).astype(BF16)
    place = extra_of(own.shape)
    extra = jnp.maximum(indicator(own == place + SLOTS), indicator(other == place + (SLOTS + EXTRA)))
    low = jnp.where(first_half(own.shape), extra, 0.0)
    high = jnp.where(first_half(own.shape), 0.0, extra)
    folds = jnp.concatenate([low, high], axis=1).astype(BF16)
    acts_copy.wait()
    acts = acts_ref[...]
    stacked = jnp.concatenate([acts[:, :half], acts[:, half:]], axis=0)
    copies = []
    for pair in range(0, runs, 2):
        start, stop = pair * run, (pair + 2) * run
        rows = dot(main[start * SLOTS : stop * SLOTS], acts)
        held[start:stop, :, :width] = rows.reshape(2 * run, SLOTS, width).astype(BF16)
        folded = dot(folds[start * SLOTS : stop * SLOTS], stacked)
        held[start:stop, :, width:] = folded.reshape(2 * run, SLOTS, half).astype(BF16)
        for part in (pair, pair + 1):
            there = pl.ds(part * run, run)
            copies.append(pltpu.make_async_copy(held.at[there], out_hbm.at[there], out_sems.at[part]))
            copies[-1].start()
    wait_all(copies)


def weight_kernel(ids_ref, gates_ref, main_ref, extra_ref):
    tokens = ids_ref.shape[1]
    experts = main_ref.shape[1] // SLOTS
    labels = iota((experts, tokens), 0)
    named = marks_of(ids_ref, labels)
    gates = jnp.zeros((experts, tokens), F32)
    for entry in range(ids_ref.shape[0]):
        value = gates_ref[entry : entry + 1, :].astype(F32)
        gates = gates + jnp.where(labels == ids_ref[entry : entry + 1, :], value, 0.0)
    ranks = jnp.where(named > 0.0, ranks_of(named), 99.0)
    own = spread(ranks, 0)
    own_gates = spread(gates, 0)
    main_ref[...] = jnp.where(own == slot_of(own.shape), own_gates, 0.0).T.astype(BF16)
    place = extra_of(own.shape)
    extra = jnp.where(own == place + SLOTS, own_gates, 0.0)
    extra += jnp.where(spread(ranks, 1) == place + (SLOTS + EXTRA), spread(gates, 1), 0.0)
    extra_ref[0] = jnp.where(first_half(own.shape), extra, 0.0).T.astype(BF16)
    extra_ref[1] = jnp.where(first_half(own.shape), 0.0, extra).T.astype(BF16)


CHUNKS = 4


def expert_loads(sources, weights, sems):
    loads = []
    for place, (source, weight) in enumerate(zip(sources, weights)):
        rows = weight.shape[0] // CHUNKS
        for part in range(CHUNKS):
            there = pl.ds(part * rows, rows)
            loads.append(pltpu.make_async_copy(source.at[0, there], weight.at[there], sems.at[place, part]))
    return loads


def expert_rows(blocks, weights, loads=None):
    gate_w, up_w, down_w = weights
    if loads:
        wait_all(loads[:CHUNKS])
    gates = [dot(rows, gate_w[...]) for rows in blocks]
    if loads:
        wait_all(loads[CHUNKS : 2 * CHUNKS])
    ups = [dot(rows, up_w[...]) for rows in blocks]
    hidden = [(g / (1.0 + jnp.exp(-g)) * u).astype(BF16) for g, u in zip(gates, ups)]
    if loads:
        wait_all(loads[2 * CHUNKS :])
    return [dot(rows, down_w[...]).astype(BF16) for rows in hidden]


def unfold(folded):
    shape = (folded.shape[0] // 2, folded.shape[0])
    row = iota(shape, 0)
    start = (row >> 2) * SLOTS + (row & (EXTRA - 1))
    low = indicator(iota(shape, 1) == start).astype(BF16)
    high = indicator(iota(shape, 1) == start + EXTRA).astype(BF16)
    return jnp.concatenate([dot(low, folded).astype(BF16), dot(high, folded).astype(BF16)], axis=1)


def fold(rows):
    half = rows.shape[1] // 2
    shape = (rows.shape[0] * 2, rows.shape[0])
    source = (iota(shape, 0) >> SHIFT) * EXTRA + (iota(shape, 0) & (EXTRA - 1))
    match = iota(shape, 1) == source
    low = indicator(match & first_half(shape)).astype(BF16)
    high = indicator(match & jnp.logical_not(first_half(shape))).astype(BF16)
    return (dot(low, rows[:, :half]) + dot(high, rows[:, half:])).astype(BF16)


def expert_kernel(mode_ref, rows_hbm, *refs):
    out_hbm, held, held_extra, done, done_extra = refs[6:11]
    weights = refs[11:14], refs[14:17]
    row_sems, out_sems, sems = refs[17:]
    blocks, count, slots, width = held.shape
    half = width // 2
    mode = mode_ref[0]

    def moves(block):
        there = pl.ds(block * count, count)
        main, extra = pl.ds(0, width), pl.ds(width, half)
        return (
            pltpu.make_async_copy(rows_hbm.at[there, :, main], held.at[block], row_sems.at[0, block]),
            pltpu.make_async_copy(rows_hbm.at[there, :, extra], held_extra.at[block], row_sems.at[1, block]),
            pltpu.make_async_copy(done.at[block], out_hbm.at[there, :, main], out_sems.at[0, block]),
            pltpu.make_async_copy(done_extra.at[block], out_hbm.at[there, :, extra], out_sems.at[1, block]),
        )

    rows, extra_rows, stores, extra_stores = zip(*[moves(block) for block in range(blocks)])
    loads = [expert_loads(refs[3 * side : 3 * side + 3], weights[side], sems.at[side]) for side in range(2)]
    for copy in [*rows[:2], *loads[0][: 2 * CHUNKS], *rows[2:], *loads[0][2 * CHUNKS :], *extra_rows]:
        copy.start()

    @pl.when(mode == 0)
    def _():
        done_extra[...] = jnp.zeros(done_extra.shape, BF16)
        for store in extra_stores:
            store.start()

    for pair in range(0, blocks, 2):
        wait_all(rows[pair : pair + 2])
        both = [held[block].reshape(count * slots, width) for block in (pair, pair + 1)]
        results = expert_rows(both, weights[0], loads[0] if pair == 0 else None)
        for block, result in zip((pair, pair + 1), results):
            done[block] = result.reshape(count, slots, width)
            stores[block].start()
        if pair == 0:

            @pl.when(mode == 2)
            def _():
                for copy in loads[1]:
                    copy.start()

    wait_all(extra_rows)

    def extras(side):
        if side:
            wait_all(loads[1])
        parts = [unfold(held_extra[block].reshape(count * slots, half)) for block in range(blocks)]
        both = [jnp.concatenate(parts[a : a + 2], axis=0) for a in range(0, blocks, 2)]
        results = expert_rows(both, weights[side])
        for block in range(blocks):
            start = (block % 2) * count * EXTRA
            result = results[block // 2][start : start + count * EXTRA]
            done_extra[block] = fold(result).reshape(count, slots, half)
            extra_stores[block].start()

    for side in range(2):

        @pl.when(mode == side + 1)
        def _():
            extras(side)

    wait_all(stores + extra_stores)


def combine_kernel(main_w_hbm, extra_w_hbm, rows_hbm, out_hbm, main_w, extra_w, held, out_ref, w_sems, sems, out_sems):
    tokens, width = out_ref.shape
    half = width // 2
    runs = sems.shape[0]
    run = held.shape[0] // runs
    w_copies = [
        pltpu.make_async_copy(main_w_hbm, main_w, w_sems.at[0]),
        pltpu.make_async_copy(extra_w_hbm, extra_w, w_sems.at[1]),
    ]
    copies = [
        pltpu.make_async_copy(rows_hbm.at[pl.ds(part * run, run)], held.at[pl.ds(part * run, run)], sems.at[part])
        for part in range(runs)
    ]
    for copy in w_copies + copies:
        copy.start()
    wait_all(w_copies)
    totals = [None, None]
    for pair in range(0, runs, 2):
        wait_all(copies[pair : pair + 2])
        here = slice(pair * run, (pair + 2) * run)
        extra = held[here, width:]
        for side in range(2):
            rows = held[here, side * half : (side + 1) * half]
            part = dot(main_w[:, here], rows) + dot(extra_w[side, :, here], extra)
            totals[side] = part if totals[side] is None else totals[side] + part
    stores = []
    for side in range(2):
        columns = pl.ds(side * half, half)
        out_ref[:, side * half : (side + 1) * half] = totals[side].astype(BF16)
        stores.append(pltpu.make_async_copy(out_ref.at[:, columns], out_hbm.at[:, columns], out_sems.at[side]))
        stores[-1].start()
    wait_all(stores)


def params(megabytes):
    return pltpu.CompilerParams(vmem_limit_bytes=megabytes * 1024 * 1024)


def whole():
    return pl.BlockSpec(memory_space=pltpu.VMEM)


def hbm():
    return pl.BlockSpec(memory_space=pltpu.HBM)


def shards(activations, expert_ids, route_gates, gate_proj, up_proj, down_proj):
    tokens, width = activations.shape
    top = expert_ids.shape[1]
    hidden = gate_proj.shape[2]
    groups = lax.axis_size("node")
    per_group = lax.axis_size("local")
    experts = groups * per_group
    half = width // 2
    full = width + half
    my_expert = (lax.axis_index("node") * per_group + lax.axis_index("local")).astype(jnp.int32)
    id_rows = expert_ids.T
    gate_rows = route_gates.T

    sent = pl.pallas_call(
        send_kernel,
        in_specs=[hbm(), hbm()],
        out_specs=hbm(),
        out_shape=jax.ShapeDtypeStruct((experts, SLOTS, full), BF16),
        scratch_shapes=[
            pltpu.VMEM((top, tokens), jnp.int32),
            pltpu.VMEM((tokens, width), BF16),
            pltpu.VMEM((experts, SLOTS, full), BF16),
            pltpu.SemaphoreType.DMA((2,)),
            pltpu.SemaphoreType.DMA((8,)),
        ],
        compiler_params=params(60),
        name="send_rows",
    )(id_rows, activations)

    def exchange(rows):
        return lax.all_to_all(rows, ("node", "local"), split_axis=0, concat_axis=0, tiled=True)

    arrived = exchange(sent)
    cores = [(i, i ^ 1) for i in range(per_group)]
    other = [lax.ppermute(weight, "local", cores) for weight in (gate_proj, up_proj, down_proj)]

    mine = jnp.sum((expert_ids == my_expert).astype(jnp.int32)) > SLOTS
    theirs = jnp.sum((expert_ids == (my_expert ^ 1)).astype(jnp.int32)) > SLOTS
    mode = jnp.where(mine, 1, jnp.where(theirs, 2, 0)).astype(jnp.int32).reshape(1)
    count = experts * SLOTS
    weight_shapes = [(width, hidden), (width, hidden), (hidden, width)]
    results = pl.pallas_call(
        expert_kernel,
        in_specs=[pl.BlockSpec(memory_space=pltpu.SMEM), hbm()] + [hbm()] * 6,
        out_specs=hbm(),
        out_shape=jax.ShapeDtypeStruct((experts, SLOTS, full), BF16),
        scratch_shapes=[
            pltpu.VMEM((4, experts // 4, SLOTS, width), BF16),
            pltpu.VMEM((4, experts // 4, SLOTS, half), BF16),
        ]
        * 2
        + [pltpu.VMEM(shape, BF16) for shape in weight_shapes] * 2
        + [pltpu.SemaphoreType.DMA((2, 4)), pltpu.SemaphoreType.DMA((2, 4)), pltpu.SemaphoreType.DMA((2, 3, CHUNKS))],
        compiler_params=params(60),
        cost_estimate=pl.CostEstimate(
            flops=9 * count * width * hidden,
            bytes_accessed=6 * count * width + 12 * width * hidden,
            transcendentals=2 * count * hidden,
        ),
        name="expert",
    )(mode, arrived, gate_proj, up_proj, down_proj, *other)

    main_w, extra_w = pl.pallas_call(
        weight_kernel,
        in_specs=[whole(), whole()],
        out_specs=[whole(), whole()],
        out_shape=[
            jax.ShapeDtypeStruct((tokens, count), BF16),
            jax.ShapeDtypeStruct((2, tokens, count), BF16),
        ],
        compiler_params=params(24),
        name="combine_weights",
    )(id_rows, gate_rows)

    returned = exchange(results).reshape(count, full)
    return pl.pallas_call(
        combine_kernel,
        in_specs=[hbm()] * 3,
        out_specs=hbm(),
        out_shape=jax.ShapeDtypeStruct((tokens, width), BF16),
        scratch_shapes=[
            pltpu.VMEM((tokens, count), BF16),
            pltpu.VMEM((2, tokens, count), BF16),
            pltpu.VMEM((count, full), BF16),
            pltpu.VMEM((tokens, width), BF16),
            pltpu.SemaphoreType.DMA((2,)),
            pltpu.SemaphoreType.DMA((8,)),
            pltpu.SemaphoreType.DMA((2,)),
        ],
        compiler_params=params(60),
        name="combine",
    )(main_w, extra_w, returned)


def solution(mesh):
    rows = P(("node", "local"), None)
    stacks = P(("node", "local"), None, None)
    return jax.shard_map(
        shards, mesh=mesh, in_specs=(rows, rows, rows, stacks, stacks, stacks), out_specs=rows, check_vma=False
    )
```

```python
import functools

import jax
import jax.numpy as jnp
from jax import lax
from jax.experimental import pallas as pl
from jax.experimental.pallas import tpu as pltpu
from jax.sharding import PartitionSpec as P

SLOTS = 8
EXTRA = 4
SHIFT = 3
BF16 = jnp.bfloat16
F32 = jnp.float32


def iota(shape, dim):
    return lax.broadcasted_iota(jnp.int32, shape, dim)


def indicator(mask):
    return jnp.where(mask, 1.0, 0.0).astype(F32)


def dot(left, right):
    return jnp.dot(left, right, preferred_element_type=F32)


def ranks_of(named):
    tokens = named.shape[1]
    earlier = indicator(iota((tokens, tokens), 0) < iota((tokens, tokens), 1))
    return dot(named.astype(BF16), earlier.astype(BF16))


def spread(values, flip):
    labels = values.shape[0]
    owner = (iota((labels * SLOTS, labels), 0) >> SHIFT) ^ flip
    picks = indicator(owner == iota((labels * SLOTS, labels), 1))
    return dot(picks.astype(BF16), values.astype(BF16))


def marks_of(ids_ref, labels):
    total = indicator(labels == ids_ref[0:1, :])
    for entry in range(1, ids_ref.shape[0]):
        total = total + indicator(labels == ids_ref[entry : entry + 1, :])
    return total


def slot_of(shape):
    return (iota(shape, 0) & (SLOTS - 1)).astype(F32)


def extra_of(shape):
    return (iota(shape, 0) & (EXTRA - 1)).astype(F32)


def first_half(shape):
    return (iota(shape, 0) & EXTRA) == 0


def wait_all(copies):
    for copy in copies:
        copy.wait()


def send_kernel(ids_hbm, acts_hbm, out_hbm, ids_ref, acts_ref, held, in_sems, out_sems):
    tokens, width = acts_ref.shape
    experts = held.shape[0]
    half = width // 2
    runs = out_sems.shape[0]
    run = experts // runs
    ids_copy = pltpu.make_async_copy(ids_hbm, ids_ref, in_sems.at[0])
    acts_copy = pltpu.make_async_copy(acts_hbm, acts_ref, in_sems.at[1])
    ids_copy.start()
    acts_copy.start()
    ids_copy.wait()
    named = marks_of(ids_ref, iota((experts, tokens), 0))
    ranks = jnp.where(named > 0.0, ranks_of(named), 99.0)
    own = spread(ranks, 0)
    other = spread(ranks, 1)
    main = indicator(own == slot_of(own.shape)).astype(BF16)
    place = extra_of(own.shape)
    extra = jnp.maximum(indicator(own == place + SLOTS), indicator(other == place + (SLOTS + EXTRA)))
    low = jnp.where(first_half(own.shape), extra, 0.0)
    high = jnp.where(first_half(own.shape), 0.0, extra)
    folds = jnp.concatenate([low, high], axis=1).astype(BF16)
    acts_copy.wait()
    acts = acts_ref[...]
    stacked = jnp.concatenate([acts[:, :half], acts[:, half:]], axis=0)
    copies = []
    for pair in range(0, runs, 2):
        start, stop = pair * run, (pair + 2) * run
        rows = dot(main[start * SLOTS : stop * SLOTS], acts)
        held[start:stop, :, :width] = rows.reshape(2 * run, SLOTS, width).astype(BF16)
        folded = dot(folds[start * SLOTS : stop * SLOTS], stacked)
        held[start:stop, :, width:] = folded.reshape(2 * run, SLOTS, half).astype(BF16)
        for part in (pair, pair + 1):
            there = pl.ds(part * run, run)
            copies.append(pltpu.make_async_copy(held.at[there], out_hbm.at[there], out_sems.at[part]))
            copies[-1].start()
    wait_all(copies)


def weight_kernel(ids_ref, gates_ref, main_ref, extra_ref):
    tokens = ids_ref.shape[1]
    experts = main_ref.shape[1] // SLOTS
    labels = iota((experts, tokens), 0)
    named = marks_of(ids_ref, labels)
    gates = jnp.zeros((experts, tokens), F32)
    for entry in range(ids_ref.shape[0]):
        value = gates_ref[entry : entry + 1, :].astype(F32)
        gates = gates + jnp.where(labels == ids_ref[entry : entry + 1, :], value, 0.0)
    ranks = jnp.where(named > 0.0, ranks_of(named), 99.0)
    own = spread(ranks, 0)
    own_gates = spread(gates, 0)
    main_ref[...] = jnp.where(own == slot_of(own.shape), own_gates, 0.0).T.astype(BF16)
    place = extra_of(own.shape)
    extra = jnp.where(own == place + SLOTS, own_gates, 0.0)
    extra += jnp.where(spread(ranks, 1) == place + (SLOTS + EXTRA), spread(gates, 1), 0.0)
    extra_ref[0] = jnp.where(first_half(own.shape), extra, 0.0).T.astype(BF16)
    extra_ref[1] = jnp.where(first_half(own.shape), 0.0, extra).T.astype(BF16)


CHUNKS = 8


def expert_loads(sources, weights, sems):
    loads = []
    for place, (source, weight) in enumerate(zip(sources, weights)):
        rows = weight.shape[0] // CHUNKS
        for part in range(CHUNKS):
            there = pl.ds(part * rows, rows)
            loads.append(pltpu.make_async_copy(source.at[0, there], weight.at[there], sems.at[place, part]))
    return loads


def arriving(blocks, weight, loads):
    parts = 2
    run = weight.shape[0] // parts
    totals = [None] * len(blocks)
    for part in range(parts):
        wait_all(loads[part * CHUNKS // parts : (part + 1) * CHUNKS // parts])
        here = slice(part * run, (part + 1) * run)
        outs = [dot(rows[:, here], weight[here]) for rows in blocks]
        totals = [out if total is None else total + out for total, out in zip(totals, outs)]
    return totals


def expert_rows(blocks, weights, loads=None):
    gate_w, up_w, down_w = weights
    if loads:
        gates = arriving(blocks, gate_w, loads[:CHUNKS])
        ups = arriving(blocks, up_w, loads[CHUNKS : 2 * CHUNKS])
    else:
        gates = [dot(rows, gate_w[...]) for rows in blocks]
        ups = [dot(rows, up_w[...]) for rows in blocks]
    hidden = [(g / (1.0 + jnp.exp(-g)) * u).astype(BF16) for g, u in zip(gates, ups)]
    if loads:
        wait_all(loads[2 * CHUNKS :])
    return [dot(rows, down_w[...]).astype(BF16) for rows in hidden]


def unfold(folded):
    shape = (folded.shape[0] // 2, folded.shape[0])
    row = iota(shape, 0)
    start = (row >> 2) * SLOTS + (row & (EXTRA - 1))
    low = indicator(iota(shape, 1) == start).astype(BF16)
    high = indicator(iota(shape, 1) == start + EXTRA).astype(BF16)
    return jnp.concatenate([dot(low, folded).astype(BF16), dot(high, folded).astype(BF16)], axis=1)


def fold(rows):
    half = rows.shape[1] // 2
    shape = (rows.shape[0] * 2, rows.shape[0])
    source = (iota(shape, 0) >> SHIFT) * EXTRA + (iota(shape, 0) & (EXTRA - 1))
    match = iota(shape, 1) == source
    low = indicator(match & first_half(shape)).astype(BF16)
    high = indicator(match & jnp.logical_not(first_half(shape))).astype(BF16)
    return (dot(low, rows[:, :half]) + dot(high, rows[:, half:])).astype(BF16)


def expert_kernel(mode_ref, rows_hbm, *refs):
    out_hbm, held, held_extra, done, done_extra = refs[6:11]
    weights = refs[11:14], refs[14:17]
    row_sems, out_sems, sems = refs[17:]
    blocks, count, slots, width = held.shape
    half = width // 2
    mode = mode_ref[0]

    def moves(block):
        there = pl.ds(block * count, count)
        main, extra = pl.ds(0, width), pl.ds(width, half)
        return (
            pltpu.make_async_copy(rows_hbm.at[there, :, main], held.at[block], row_sems.at[0, block]),
            pltpu.make_async_copy(rows_hbm.at[there, :, extra], held_extra.at[block], row_sems.at[1, block]),
            pltpu.make_async_copy(done.at[block], out_hbm.at[there, :, main], out_sems.at[0, block]),
            pltpu.make_async_copy(done_extra.at[block], out_hbm.at[there, :, extra], out_sems.at[1, block]),
        )

    rows, extra_rows, stores, extra_stores = zip(*[moves(block) for block in range(blocks)])
    loads = [expert_loads(refs[3 * side : 3 * side + 3], weights[side], sems.at[side]) for side in range(2)]
    for copy in [*rows[:2], *loads[0][: 2 * CHUNKS], *rows[2:], *loads[0][2 * CHUNKS :], *extra_rows]:
        copy.start()

    @pl.when(mode == 0)
    def _():
        done_extra[...] = jnp.zeros(done_extra.shape, BF16)
        for store in extra_stores:
            store.start()

    for pair in range(0, blocks, 2):
        wait_all(rows[pair : pair + 2])
        both = [held[block].reshape(count * slots, width) for block in (pair, pair + 1)]
        results = expert_rows(both, weights[0], loads[0] if pair == 0 else None)
        for block, result in zip((pair, pair + 1), results):
            done[block] = result.reshape(count, slots, width)
            stores[block].start()
        if pair == 0:

            @pl.when(mode == 2)
            def _():
                for copy in loads[1]:
                    copy.start()

    wait_all(extra_rows)

    def extras(side):
        if side:
            wait_all(loads[1])
        parts = [unfold(held_extra[block].reshape(count * slots, half)) for block in range(blocks)]
        both = [jnp.concatenate(parts[a : a + 2], axis=0) for a in range(0, blocks, 2)]
        results = expert_rows(both, weights[side])
        for block in range(blocks):
            start = (block % 2) * count * EXTRA
            result = results[block // 2][start : start + count * EXTRA]
            done_extra[block] = fold(result).reshape(count, slots, half)
            extra_stores[block].start()

    for side in range(2):

        @pl.when(mode == side + 1)
        def _():
            extras(side)

    wait_all(stores + extra_stores)


def combine_kernel(main_w_hbm, extra_w_hbm, rows_hbm, out_hbm, main_w, extra_w, held, out_ref, w_sems, sems, out_sems):
    tokens, width = out_ref.shape
    half = width // 2
    runs = sems.shape[0]
    run = held.shape[0] // runs
    w_copies = [
        pltpu.make_async_copy(main_w_hbm, main_w, w_sems.at[0]),
        pltpu.make_async_copy(extra_w_hbm, extra_w, w_sems.at[1]),
    ]
    copies = [
        pltpu.make_async_copy(rows_hbm.at[pl.ds(part * run, run)], held.at[pl.ds(part * run, run)], sems.at[part])
        for part in range(runs)
    ]
    for copy in w_copies + copies:
        copy.start()
    wait_all(w_copies)
    totals = [None, None]
    for first in range(0, runs, 4):
        wait_all(copies[first : first + 4])
        here = slice(first * run, (first + 4) * run)
        extra = held[here, width:]
        for side in range(2):
            rows = held[here, side * half : (side + 1) * half]
            part = dot(main_w[:, here], rows) + dot(extra_w[side, :, here], extra)
            totals[side] = part if totals[side] is None else totals[side] + part
    stores = []
    for side in range(2):
        columns = pl.ds(side * half, half)
        out_ref[:, side * half : (side + 1) * half] = totals[side].astype(BF16)
        stores.append(pltpu.make_async_copy(out_ref.at[:, columns], out_hbm.at[:, columns], out_sems.at[side]))
        stores[-1].start()
    wait_all(stores)


def params(megabytes):
    return pltpu.CompilerParams(vmem_limit_bytes=megabytes * 1024 * 1024)


def whole():
    return pl.BlockSpec(memory_space=pltpu.VMEM)


def hbm():
    return pl.BlockSpec(memory_space=pltpu.HBM)


def shards(activations, expert_ids, route_gates, gate_proj, up_proj, down_proj):
    tokens, width = activations.shape
    top = expert_ids.shape[1]
    hidden = gate_proj.shape[2]
    groups = lax.axis_size("node")
    per_group = lax.axis_size("local")
    experts = groups * per_group
    half = width // 2
    full = width + half
    my_expert = (lax.axis_index("node") * per_group + lax.axis_index("local")).astype(jnp.int32)
    id_rows = expert_ids.T
    gate_rows = route_gates.T

    sent = pl.pallas_call(
        send_kernel,
        in_specs=[hbm(), hbm()],
        out_specs=hbm(),
        out_shape=jax.ShapeDtypeStruct((experts, SLOTS, full), BF16),
        scratch_shapes=[
            pltpu.VMEM((top, tokens), jnp.int32),
            pltpu.VMEM((tokens, width), BF16),
            pltpu.VMEM((experts, SLOTS, full), BF16),
            pltpu.SemaphoreType.DMA((2,)),
            pltpu.SemaphoreType.DMA((8,)),
        ],
        compiler_params=params(60),
        name="send_rows",
    )(id_rows, activations)

    def exchange(rows):
        return lax.all_to_all(rows, ("node", "local"), split_axis=0, concat_axis=0, tiled=True)

    arrived = exchange(sent)
    cores = [(i, i ^ 1) for i in range(per_group)]
    other = [lax.ppermute(weight, "local", cores) for weight in (gate_proj, up_proj, down_proj)]

    mine = jnp.sum((expert_ids == my_expert).astype(jnp.int32)) > SLOTS
    theirs = jnp.sum((expert_ids == (my_expert ^ 1)).astype(jnp.int32)) > SLOTS
    mode = jnp.where(mine, 1, jnp.where(theirs, 2, 0)).astype(jnp.int32).reshape(1)
    count = experts * SLOTS
    weight_shapes = [(width, hidden), (width, hidden), (hidden, width)]
    results = pl.pallas_call(
        expert_kernel,
        in_specs=[pl.BlockSpec(memory_space=pltpu.SMEM), hbm()] + [hbm()] * 6,
        out_specs=hbm(),
        out_shape=jax.ShapeDtypeStruct((experts, SLOTS, full), BF16),
        scratch_shapes=[
            pltpu.VMEM((4, experts // 4, SLOTS, width), BF16),
            pltpu.VMEM((4, experts // 4, SLOTS, half), BF16),
        ]
        * 2
        + [pltpu.VMEM(shape, BF16) for shape in weight_shapes] * 2
        + [pltpu.SemaphoreType.DMA((2, 4)), pltpu.SemaphoreType.DMA((2, 4)), pltpu.SemaphoreType.DMA((2, 3, CHUNKS))],
        compiler_params=params(60),
        cost_estimate=pl.CostEstimate(
            flops=9 * count * width * hidden,
            bytes_accessed=6 * count * width + 12 * width * hidden,
            transcendentals=2 * count * hidden,
        ),
        name="expert",
    )(mode, arrived, gate_proj, up_proj, down_proj, *other)

    main_w, extra_w = pl.pallas_call(
        weight_kernel,
        in_specs=[whole(), whole()],
        out_specs=[whole(), whole()],
        out_shape=[
            jax.ShapeDtypeStruct((tokens, count), BF16),
            jax.ShapeDtypeStruct((2, tokens, count), BF16),
        ],
        compiler_params=params(24),
        name="combine_weights",
    )(id_rows, gate_rows)

    returned = exchange(results).reshape(count, full)
    return pl.pallas_call(
        combine_kernel,
        in_specs=[hbm()] * 3,
        out_specs=hbm(),
        out_shape=jax.ShapeDtypeStruct((tokens, width), BF16),
        scratch_shapes=[
            pltpu.VMEM((tokens, count), BF16),
            pltpu.VMEM((2, tokens, count), BF16),
            pltpu.VMEM((count, full), BF16),
            pltpu.VMEM((tokens, width), BF16),
            pltpu.SemaphoreType.DMA((2,)),
            pltpu.SemaphoreType.DMA((16,)),
            pltpu.SemaphoreType.DMA((2,)),
        ],
        compiler_params=params(60),
        name="combine",
    )(main_w, extra_w, returned)


def solution(mesh):
    rows = P(("node", "local"), None)
    stacks = P(("node", "local"), None, None)
    return jax.shard_map(
        shards, mesh=mesh, in_specs=(rows, rows, rows, stacks, stacks, stacks), out_specs=rows, check_vma=False
    )
```

```python
import functools

import jax
import jax.numpy as jnp
from jax import lax
from jax.experimental import pallas as pl
from jax.experimental.pallas import tpu as pltpu
from jax.sharding import PartitionSpec as P

SLOTS = 8
EXTRA = 4
SHIFT = 3
BF16 = jnp.bfloat16
F32 = jnp.float32


def iota(shape, dim):
    return lax.broadcasted_iota(jnp.int32, shape, dim)


def indicator(mask):
    return jnp.where(mask, 1.0, 0.0).astype(F32)


def dot(left, right):
    return jnp.dot(left, right, preferred_element_type=F32)


def ranks_of(named):
    tokens = named.shape[1]
    earlier = indicator(iota((tokens, tokens), 0) < iota((tokens, tokens), 1))
    return dot(named.astype(BF16), earlier.astype(BF16))


def spread(values, flip):
    labels = values.shape[0]
    owner = (iota((labels * SLOTS, labels), 0) >> SHIFT) ^ flip
    picks = indicator(owner == iota((labels * SLOTS, labels), 1))
    return dot(picks.astype(BF16), values.astype(BF16))


def marks_of(ids_ref, labels):
    total = indicator(labels == ids_ref[0:1, :])
    for entry in range(1, ids_ref.shape[0]):
        total = total + indicator(labels == ids_ref[entry : entry + 1, :])
    return total


def slot_of(shape):
    return (iota(shape, 0) & (SLOTS - 1)).astype(F32)


def extra_of(shape):
    return (iota(shape, 0) & (EXTRA - 1)).astype(F32)


def first_half(shape):
    return (iota(shape, 0) & EXTRA) == 0


def wait_all(copies):
    for copy in copies:
        copy.wait()


def send_kernel(ids_hbm, acts_hbm, out_hbm, ids_ref, acts_ref, held, in_sems, out_sems):
    tokens, width = acts_ref.shape
    experts = held.shape[0]
    half = width // 2
    runs = out_sems.shape[0]
    run = experts // runs
    ids_copy = pltpu.make_async_copy(ids_hbm, ids_ref, in_sems.at[0])
    acts_copy = pltpu.make_async_copy(acts_hbm, acts_ref, in_sems.at[1])
    ids_copy.start()
    acts_copy.start()
    ids_copy.wait()
    named = marks_of(ids_ref, iota((experts, tokens), 0))
    ranks = jnp.where(named > 0.0, ranks_of(named), 99.0)
    own = spread(ranks, 0)
    other = spread(ranks, 1)
    main = indicator(own == slot_of(own.shape)).astype(BF16)
    place = extra_of(own.shape)
    extra = jnp.maximum(indicator(own == place + SLOTS), indicator(other == place + (SLOTS + EXTRA)))
    low = jnp.where(first_half(own.shape), extra, 0.0)
    high = jnp.where(first_half(own.shape), 0.0, extra)
    folds = jnp.concatenate([low, high], axis=1).astype(BF16)
    acts_copy.wait()
    acts = acts_ref[...]
    stacked = jnp.concatenate([acts[:, :half], acts[:, half:]], axis=0)
    copies = []
    for pair in range(0, runs, 2):
        start, stop = pair * run, (pair + 2) * run
        rows = dot(main[start * SLOTS : stop * SLOTS], acts)
        held[start:stop, :, :width] = rows.reshape(2 * run, SLOTS, width).astype(BF16)
        folded = dot(folds[start * SLOTS : stop * SLOTS], stacked)
        held[start:stop, :, width:] = folded.reshape(2 * run, SLOTS, half).astype(BF16)
        for part in (pair, pair + 1):
            there = pl.ds(part * run, run)
            copies.append(pltpu.make_async_copy(held.at[there], out_hbm.at[there], out_sems.at[part]))
            copies[-1].start()
    wait_all(copies)


def weight_kernel(ids_ref, gates_ref, main_ref, extra_ref):
    tokens = ids_ref.shape[1]
    experts = main_ref.shape[1] // SLOTS
    labels = iota((experts, tokens), 0)
    named = marks_of(ids_ref, labels)
    gates = jnp.zeros((experts, tokens), F32)
    for entry in range(ids_ref.shape[0]):
        value = gates_ref[entry : entry + 1, :].astype(F32)
        gates = gates + jnp.where(labels == ids_ref[entry : entry + 1, :], value, 0.0)
    ranks = jnp.where(named > 0.0, ranks_of(named), 99.0)
    own = spread(ranks, 0)
    own_gates = spread(gates, 0)
    main_ref[...] = jnp.where(own == slot_of(own.shape), own_gates, 0.0).T.astype(BF16)
    place = extra_of(own.shape)
    extra = jnp.where(own == place + SLOTS, own_gates, 0.0)
    extra += jnp.where(spread(ranks, 1) == place + (SLOTS + EXTRA), spread(gates, 1), 0.0)
    extra_ref[0] = jnp.where(first_half(own.shape), extra, 0.0).T.astype(BF16)
    extra_ref[1] = jnp.where(first_half(own.shape), 0.0, extra).T.astype(BF16)


CHUNKS = 2


def expert_loads(sources, weights, sems):
    loads = []
    for place, (source, weight) in enumerate(zip(sources, weights)):
        rows = weight.shape[0] // CHUNKS
        for part in range(CHUNKS):
            there = pl.ds(part * rows, rows)
            loads.append(pltpu.make_async_copy(source.at[0, there], weight.at[there], sems.at[place, part]))
    return loads


def expert_rows(blocks, weights, loads=None):
    gate_w, up_w, down_w = weights
    if loads:
        wait_all(loads[:CHUNKS])
    gates = [dot(rows, gate_w[...]) for rows in blocks]
    if loads:
        wait_all(loads[CHUNKS : 2 * CHUNKS])
    ups = [dot(rows, up_w[...]) for rows in blocks]
    hidden = [(g / (1.0 + jnp.exp(-g)) * u).astype(BF16) for g, u in zip(gates, ups)]
    if loads:
        wait_all(loads[2 * CHUNKS :])
    return [dot(rows, down_w[...]).astype(BF16) for rows in hidden]


def unfold(folded):
    shape = (folded.shape[0] // 2, folded.shape[0])
    row = iota(shape, 0)
    start = (row >> 2) * SLOTS + (row & (EXTRA - 1))
    low = indicator(iota(shape, 1) == start).astype(BF16)
    high = indicator(iota(shape, 1) == start + EXTRA).astype(BF16)
    return jnp.concatenate([dot(low, folded).astype(BF16), dot(high, folded).astype(BF16)], axis=1)


def fold(rows):
    half = rows.shape[1] // 2
    shape = (rows.shape[0] * 2, rows.shape[0])
    source = (iota(shape, 0) >> SHIFT) * EXTRA + (iota(shape, 0) & (EXTRA - 1))
    match = iota(shape, 1) == source
    low = indicator(match & first_half(shape)).astype(BF16)
    high = indicator(match & jnp.logical_not(first_half(shape))).astype(BF16)
    return (dot(low, rows[:, :half]) + dot(high, rows[:, half:])).astype(BF16)


def expert_kernel(mode_ref, rows_hbm, *refs):
    out_hbm, held, held_extra, done, done_extra = refs[6:11]
    weights = refs[11:14], refs[14:17]
    row_sems, out_sems, sems = refs[17:]
    blocks, count, slots, width = held.shape
    half = width // 2
    mode = mode_ref[0]

    def moves(block):
        there = pl.ds(block * count, count)
        main, extra = pl.ds(0, width), pl.ds(width, half)
        return (
            pltpu.make_async_copy(rows_hbm.at[there, :, main], held.at[block], row_sems.at[0, block]),
            pltpu.make_async_copy(rows_hbm.at[there, :, extra], held_extra.at[block], row_sems.at[1, block]),
            pltpu.make_async_copy(done.at[block], out_hbm.at[there, :, main], out_sems.at[0, block]),
            pltpu.make_async_copy(done_extra.at[block], out_hbm.at[there, :, extra], out_sems.at[1, block]),
        )

    rows, extra_rows, stores, extra_stores = zip(*[moves(block) for block in range(blocks)])
    loads = [expert_loads(refs[3 * side : 3 * side + 3], weights[side], sems.at[side]) for side in range(2)]
    for copy in [*rows[:2], *loads[0][: 2 * CHUNKS], *rows[2:], *loads[0][2 * CHUNKS :], *extra_rows]:
        copy.start()

    @pl.when(mode == 0)
    def _():
        done_extra[...] = jnp.zeros(done_extra.shape, BF16)
        for store in extra_stores:
            store.start()

    for pair in range(0, blocks, 2):
        wait_all(rows[pair : pair + 2])
        both = [held[block].reshape(count * slots, width) for block in (pair, pair + 1)]
        results = expert_rows(both, weights[0], loads[0] if pair == 0 else None)
        for block, result in zip((pair, pair + 1), results):
            done[block] = result.reshape(count, slots, width)
            stores[block].start()
        if pair == 0:

            @pl.when(mode == 2)
            def _():
                for copy in loads[1]:
                    copy.start()

    wait_all(extra_rows)

    def extras(side):
        if side:
            wait_all(loads[1])
        parts = [unfold(held_extra[block].reshape(count * slots, half)) for block in range(blocks)]
        both = [jnp.concatenate(parts[a : a + 2], axis=0) for a in range(0, blocks, 2)]
        results = expert_rows(both, weights[side])
        for block in range(blocks):
            start = (block % 2) * count * EXTRA
            result = results[block // 2][start : start + count * EXTRA]
            done_extra[block] = fold(result).reshape(count, slots, half)
            extra_stores[block].start()

    for side in range(2):

        @pl.when(mode == side + 1)
        def _():
            extras(side)

    wait_all(stores + extra_stores)


def combine_kernel(main_w_hbm, extra_w_hbm, rows_hbm, out_hbm, main_w, extra_w, held, out_ref, w_sems, sems, out_sems):
    tokens, width = out_ref.shape
    half = width // 2
    runs = sems.shape[0]
    run = held.shape[0] // runs
    w_copies = [
        pltpu.make_async_copy(main_w_hbm, main_w, w_sems.at[0]),
        pltpu.make_async_copy(extra_w_hbm, extra_w, w_sems.at[1]),
    ]
    copies = [
        pltpu.make_async_copy(rows_hbm.at[pl.ds(part * run, run)], held.at[pl.ds(part * run, run)], sems.at[part])
        for part in range(runs)
    ]
    for copy in w_copies + copies:
        copy.start()
    wait_all(w_copies)
    totals = [None, None]
    for pair in range(0, runs, 2):
        wait_all(copies[pair : pair + 2])
        here = slice(pair * run, (pair + 2) * run)
        extra = held[here, width:]
        for side in range(2):
            rows = held[here, side * half : (side + 1) * half]
            part = dot(main_w[:, here], rows) + dot(extra_w[side, :, here], extra)
            totals[side] = part if totals[side] is None else totals[side] + part
    stores = []
    for side in range(2):
        columns = pl.ds(side * half, half)
        out_ref[:, side * half : (side + 1) * half] = totals[side].astype(BF16)
        stores.append(pltpu.make_async_copy(out_ref.at[:, columns], out_hbm.at[:, columns], out_sems.at[side]))
        stores[-1].start()
    wait_all(stores)


def params(megabytes):
    return pltpu.CompilerParams(vmem_limit_bytes=megabytes * 1024 * 1024)


def whole():
    return pl.BlockSpec(memory_space=pltpu.VMEM)


def hbm():
    return pl.BlockSpec(memory_space=pltpu.HBM)


def shards(activations, expert_ids, route_gates, gate_proj, up_proj, down_proj):
    tokens, width = activations.shape
    top = expert_ids.shape[1]
    hidden = gate_proj.shape[2]
    groups = lax.axis_size("node")
    per_group = lax.axis_size("local")
    experts = groups * per_group
    half = width // 2
    full = width + half
    my_expert = (lax.axis_index("node") * per_group + lax.axis_index("local")).astype(jnp.int32)
    id_rows = expert_ids.T
    gate_rows = route_gates.T

    sent = pl.pallas_call(
        send_kernel,
        in_specs=[hbm(), hbm()],
        out_specs=hbm(),
        out_shape=jax.ShapeDtypeStruct((experts, SLOTS, full), BF16),
        scratch_shapes=[
            pltpu.VMEM((top, tokens), jnp.int32),
            pltpu.VMEM((tokens, width), BF16),
            pltpu.VMEM((experts, SLOTS, full), BF16),
            pltpu.SemaphoreType.DMA((2,)),
            pltpu.SemaphoreType.DMA((8,)),
        ],
        compiler_params=params(60),
        name="send_rows",
    )(id_rows, activations)

    def exchange(rows):
        return lax.all_to_all(rows, ("node", "local"), split_axis=0, concat_axis=0, tiled=True)

    arrived = exchange(sent)
    cores = [(i, i ^ 1) for i in range(per_group)]
    other = [lax.ppermute(weight, "local", cores) for weight in (gate_proj, up_proj, down_proj)]

    mine = jnp.sum((expert_ids == my_expert).astype(jnp.int32)) > SLOTS
    theirs = jnp.sum((expert_ids == (my_expert ^ 1)).astype(jnp.int32)) > SLOTS
    mode = jnp.where(mine, 1, jnp.where(theirs, 2, 0)).astype(jnp.int32).reshape(1)
    count = experts * SLOTS
    weight_shapes = [(width, hidden), (width, hidden), (hidden, width)]
    results = pl.pallas_call(
        expert_kernel,
        in_specs=[pl.BlockSpec(memory_space=pltpu.SMEM), hbm()] + [hbm()] * 6,
        out_specs=hbm(),
        out_shape=jax.ShapeDtypeStruct((experts, SLOTS, full), BF16),
        scratch_shapes=[
            pltpu.VMEM((4, experts // 4, SLOTS, width), BF16),
            pltpu.VMEM((4, experts // 4, SLOTS, half), BF16),
        ]
        * 2
        + [pltpu.VMEM(shape, BF16) for shape in weight_shapes] * 2
        + [pltpu.SemaphoreType.DMA((2, 4)), pltpu.SemaphoreType.DMA((2, 4)), pltpu.SemaphoreType.DMA((2, 3, CHUNKS))],
        compiler_params=params(60),
        cost_estimate=pl.CostEstimate(
            flops=9 * count * width * hidden,
            bytes_accessed=6 * count * width + 12 * width * hidden,
            transcendentals=2 * count * hidden,
        ),
        name="expert",
    )(mode, arrived, gate_proj, up_proj, down_proj, *other)

    main_w, extra_w = pl.pallas_call(
        weight_kernel,
        in_specs=[whole(), whole()],
        out_specs=[whole(), whole()],
        out_shape=[
            jax.ShapeDtypeStruct((tokens, count), BF16),
            jax.ShapeDtypeStruct((2, tokens, count), BF16),
        ],
        compiler_params=params(24),
        name="combine_weights",
    )(id_rows, gate_rows)

    returned = exchange(results).reshape(count, full)
    return pl.pallas_call(
        combine_kernel,
        in_specs=[hbm()] * 3,
        out_specs=hbm(),
        out_shape=jax.ShapeDtypeStruct((tokens, width), BF16),
        scratch_shapes=[
            pltpu.VMEM((tokens, count), BF16),
            pltpu.VMEM((2, tokens, count), BF16),
            pltpu.VMEM((count, full), BF16),
            pltpu.VMEM((tokens, width), BF16),
            pltpu.SemaphoreType.DMA((2,)),
            pltpu.SemaphoreType.DMA((8,)),
            pltpu.SemaphoreType.DMA((2,)),
        ],
        compiler_params=params(60),
        name="combine",
    )(main_w, extra_w, returned)


def solution(mesh):
    rows = P(("node", "local"), None)
    stacks = P(("node", "local"), None, None)
    return jax.shard_map(
        shards, mesh=mesh, in_specs=(rows, rows, rows, stacks, stacks, stacks), out_specs=rows, check_vma=False
    )
```
